32 devices in a mesh: panel: 2 (over x), lon: 8 (over z, y), colat: 2 (over core).
Axes of the slice: x: 2, y: 2, z: 4, core: 2. Of those that a mesh axis runs over, the one named last changes fastest.
Arguments:
- flow_vector: float32 [2, 3, 16, 192, 128], P('panel', None, 'colat', 'lon'), may hold values from -6 to 6
- mean_stress: float32 [2, 16, 192, 128], P('panel', 'colat', 'lon'), may hold values from -6 to 6
- shear_resistance: float32 [2, 16, 192, 128], P('panel', 'colat', 'lon'), may hold values from 0.3 to 30
- thermal_anomaly: float32 [2, 16, 192, 128], P('panel', 'colat', 'lon'), may hold values from -6 to 6
- source_azimuth_portion: int32 [2, 416], P('panel'), may hold values from 0 to 7, as said below
- source_first_slot: int32 [2, 416], P('panel'), may hold values from 0 to 166, as said below
- source_bilinear_weights: float32 [2, 2, 416], P('panel'), may hold values from 0 to 1
- source_frame_rotation: float32 [2, 416], P('panel'), may hold values from -3.140625 to 3.140625
Outputs:
- velocity_out: float32 [2, 3, 16, 192, 128], P('panel', None, 'colat', 'lon')
- pressure_out: float32 [2, 16, 192, 128], P('panel', 'colat', 'lon')
The draws below stay inside these ranges and needn't reach their ends.
Inputs may be any that keep to these rules, and one draw needn't show every extreme that they name: `source_azimuth_portion`: the donors of border row r lie in the colatitude shard of that border row. Within one colatitude shard of a panel, no longitude shard is named by more than 26 border rows, and in the first and last colatitude shard one is named exactly 26 times. Among the border rows whose ghost cells lie in one longitude shard, no longitude shard is named more than 4 times, and in the first and last colatitude shard some is named exactly 4 times. `source_first_slot`: the value v names the cell (v // 24, v mod 24) of the donor shard, with v // 24 <= 6 and v mod 24 <= 22, so that all four donor cells lie in that shard.
All inputs are finite; a program needn't handle non-finite values.
Results may differ from the reference program's by a relative error of at most 0.00002.
Values sent between devices are 32-bit elements; how exact they have to be, the bound alone decides.
A program may use at most 64 MiB of HBM per device.

```python
import math
import jax
import jax.numpy as jnp

CT = 8
CP = 24
DEPTH_LEVELS = 128
SWEEPS = 2
POLAR_CELL_COUNT = 16
AZIMUTH_COUNT = 192
ROWS = 416


def draw_source_azimuth_portion(key, part):
    lon_count = AZIMUTH_COUNT // CP
    colat_count = POLAR_CELL_COUNT // CT
    row_index = jnp.arange(ROWS, dtype=jnp.int32)
    north_offset = row_index - 2 * POLAR_CELL_COUNT
    side_row = row_index < 2 * POLAR_CELL_COUNT
    polar_index = row_index % POLAR_CELL_COUNT
    colat_group = jnp.where(side_row, polar_index // CT, jnp.where(north_offset < AZIMUTH_COUNT, 0, colat_count - 1))
    target_lon = jnp.where(row_index < POLAR_CELL_COUNT, 0, jnp.where(side_row, lon_count - 1, north_offset % AZIMUTH_COUNT // CP))
    corner_column = (target_lon == 0) | (target_lon == lon_count - 1)
    edge_group = (colat_group == 0) | (colat_group == colat_count - 1)
    natural = jnp.where(side_row, polar_index % CT, jnp.where(corner_column, CT, 0) + north_offset % CP)
    consumer_rows = jnp.where(side_row, CT + jnp.where(edge_group, CP, 0), CP + jnp.where(corner_column, CT, 0))
    panels = []
    for patch_identifier in range(2):
        panel_key = jax.random.fold_in(key, 31 + patch_identifier)
        shifts = jax.random.randint(jax.random.fold_in(panel_key, 1), (colat_count, lon_count), 0, CT + CP)
        bases = jax.random.randint(jax.random.fold_in(panel_key, 2), (colat_count,), 0, lon_count)
        turned = (natural + shifts[colat_group, target_lon]) % consumer_rows
        panels.append((bases[colat_group] + turned) % lon_count)
    return jnp.stack(panels, axis=0).astype(jnp.int32)


def draw_source_first_slot(key, part):
    polar_index = jax.random.randint(jax.random.fold_in(key, 21), (2, ROWS), 0, CT - 1)
    azimuth_index = jax.random.randint(jax.random.fold_in(key, 22), (2, ROWS), 0, CP - 1)
    donor_cells = polar_index * CP + azimuth_index
    return donor_cells.at[:, 0].set((CT - 1) * CP - 2).astype(jnp.int32)


def shard_levels(stream_key, dims, split, smallest, high):
    loudness, own = 1.0, jax.random.fold_in(stream_key, 6)
    for position, shards_of in split:
        draws = jnp.exp(jax.random.uniform(jax.random.fold_in(own, position), (shards_of,), jnp.float32, smallest / len(split), high / len(split)))
        loudness = loudness * jnp.repeat(draws, dims[position] // shards_of).reshape([-1 if axis == position else 1 for axis in range(len(dims))])
    return loudness


def scatter_about(key, extent, width, bound, cuts=(), held_as=jnp.bfloat16):
    factor_of = shard_levels(key, extent, cuts, -0.22, 0.18) if cuts else 1.0
    entries = jax.random.normal(key, extent, jnp.float32) * width * factor_of
    return jnp.minimum(jnp.maximum(entries, -bound), bound).astype(held_as)


def setup_inputs(seed: int = 0) -> dict:
    key_of = jax.random.split(jax.random.key(seed), 9)
    flow_vector = scatter_about(key_of[0], (2, 3, POLAR_CELL_COUNT, AZIMUTH_COUNT, DEPTH_LEVELS), 1.0, 6.0, ((0, 2), (2, 2), (3, 8)), jnp.float32)
    mean_stress = scatter_about(key_of[1], (2, POLAR_CELL_COUNT, AZIMUTH_COUNT, DEPTH_LEVELS), 1.0, 6.0, ((0, 2), (1, 2), (2, 8)), jnp.float32)
    shear_resistance = jnp.clip(jnp.exp(math.log(30.0) - 4.6051701 * jax.random.uniform(key_of[2], (2, POLAR_CELL_COUNT, AZIMUTH_COUNT, DEPTH_LEVELS), jnp.float32) ** shard_levels(key_of[2], (2, POLAR_CELL_COUNT, AZIMUTH_COUNT, DEPTH_LEVELS), ((0, 2), (1, 2), (2, 8)), -0.2, 0.2)), 0.3, 30.0)
    thermal_anomaly = scatter_about(key_of[3], (2, POLAR_CELL_COUNT, AZIMUTH_COUNT, DEPTH_LEVELS), 1.0, 6.0, ((0, 2), (1, 2), (2, 8)), jnp.float32)
    source_azimuth_portion = draw_source_azimuth_portion(jax.random.fold_in(key_of[8], 71), 0)
    source_first_slot = draw_source_first_slot(jax.random.fold_in(key_of[8], 71), 0)
    source_bilinear_weights = jnp.clip(1.0 * jax.random.uniform(key_of[6], (2, 2, ROWS), jnp.float32) ** shard_levels(key_of[6], (2, 2, ROWS), ((0, 2),), -0.2, 0.2), 0.0, 1.0)
    source_frame_rotation = jnp.clip(jax.random.uniform(key_of[7], (2, ROWS), jnp.float32, -3.140625, 3.140625), -3.140625, 3.140625)
    return {"flow_vector": flow_vector, "mean_stress": mean_stress, "shear_resistance": shear_resistance, "thermal_anomaly": thermal_anomaly, "source_azimuth_portion": source_azimuth_portion, "source_first_slot": source_first_slot, "source_bilinear_weights": source_bilinear_weights, "source_frame_rotation": source_frame_rotation}


OMEGA_VELOCITY = 0.8
OMEGA_PRESSURE = 0.1
INNER_RATIO = 11.0 / 9.0


def shift_up(values):
    return jnp.concatenate([values[..., 1:], jnp.zeros_like(values[..., :1])], axis=-1)


def shift_down(values):
    return jnp.concatenate([jnp.zeros_like(values[..., :1]), values[..., :-1]], axis=-1)


def blend_rotate(corner_first, corner_east, corner_south, corner_last, along_polar, along_azimuth, turn_angle):
    weight_polar = along_polar[None, :, None]
    weight_azimuth = along_azimuth[None, :, None]
    blended = (((1.0 - weight_polar) * (1.0 - weight_azimuth)) * corner_first
               + ((1.0 - weight_polar) * weight_azimuth) * corner_east
               + (weight_polar * (1.0 - weight_azimuth)) * corner_south
               + (weight_polar * weight_azimuth) * corner_last)
    cosine_turn = jnp.cos(turn_angle)[:, None]
    sine_turn = jnp.sin(turn_angle)[:, None]
    polar_part = cosine_turn * blended[1] + sine_turn * blended[2]
    azimuth_part = cosine_turn * blended[2] - sine_turn * blended[1]
    return jnp.concatenate([blended[:1], polar_part[None], azimuth_part[None], blended[3:]], axis=0)


def weighted_smoothing_pass(vel_pad, pres_pad, viscosity_padded, buoyant_temp, colatitude_value, inner_shell_radius, colatitude_spacing, longitude_spacing):
    radial_count = vel_pad.shape[-1]
    radius = inner_shell_radius + jnp.arange(radial_count, dtype=jnp.float32) + 0.5
    sine_values = jnp.sin(colatitude_value)
    sine_centre = sine_values[1:-1][:, None, None]
    sine_north = jnp.sin(colatitude_value[1:-1] - 0.5 * colatitude_spacing)[:, None, None]
    sine_south = jnp.sin(colatitude_value[1:-1] + 0.5 * colatitude_spacing)[:, None, None]
    visc_centre = viscosity_padded[1:-1, 1:-1]
    visc_above = jnp.concatenate([visc_centre[..., 1:], visc_centre[..., -1:]], axis=-1)
    visc_below = jnp.concatenate([visc_centre[..., :1], visc_centre[..., :-1]], axis=-1)
    polar_step = radius * colatitude_spacing
    azimuth_step = radius * sine_centre * longitude_spacing
    coef_above = 0.5 * (visc_centre + visc_above) * ((radius + 0.5) / radius) ** 2
    coef_below = 0.5 * (visc_centre + visc_below) * ((radius - 0.5) / radius) ** 2
    coef_north = 0.5 * (visc_centre + viscosity_padded[:-2, 1:-1]) * (sine_north / sine_centre) / polar_step ** 2
    coef_south = 0.5 * (visc_centre + viscosity_padded[2:, 1:-1]) * (sine_south / sine_centre) / polar_step ** 2
    coef_west = 0.5 * (visc_centre + viscosity_padded[1:-1, :-2]) / azimuth_step ** 2
    coef_east = 0.5 * (visc_centre + viscosity_padded[1:-1, 2:]) / azimuth_step ** 2
    diagonal = coef_above + coef_below + coef_north + coef_south + coef_west + coef_east
    pres_centre = pres_pad[1:-1, 1:-1]
    grad_radial = 0.5 * (shift_up(pres_centre) - shift_down(pres_centre))
    grad_polar = 0.5 * (pres_pad[2:, 1:-1] - pres_pad[:-2, 1:-1]) / polar_step
    grad_azimuth = 0.5 * (pres_pad[1:-1, 2:] - pres_pad[1:-1, :-2]) / azimuth_step
    forcing = (buoyant_temp - grad_radial, -grad_polar, -grad_azimuth)
    updated = []
    for component in range(3):
        field_pad = vel_pad[component]
        centre = field_pad[1:-1, 1:-1]
        viscous = (coef_above * (shift_up(centre) - centre) + coef_below * (shift_down(centre) - centre)
                   + coef_north * (field_pad[:-2, 1:-1] - centre) + coef_south * (field_pad[2:, 1:-1] - centre)
                   + coef_west * (field_pad[1:-1, :-2] - centre) + coef_east * (field_pad[1:-1, 2:] - centre))
        updated.append(centre + OMEGA_VELOCITY * (forcing[component] + viscous) / diagonal)
    radial_vel = vel_pad[0, 1:-1, 1:-1]
    div_radial = 0.5 * ((radius + 1.0) ** 2 * shift_up(radial_vel) - (radius - 1.0) ** 2 * shift_down(radial_vel)) / radius ** 2
    div_polar = 0.5 * (sine_values[2:, None, None] * vel_pad[1, 2:, 1:-1] - sine_values[:-2, None, None] * vel_pad[1, :-2, 1:-1]) / (polar_step * sine_centre)
    div_azimuth = 0.5 * (vel_pad[2, 1:-1, 2:] - vel_pad[2, 1:-1, :-2]) / azimuth_step
    divergence = div_radial + div_polar + div_azimuth
    smoothed_mean_stress = pres_centre - OMEGA_PRESSURE * visc_centre * divergence
    return jnp.stack(updated, axis=0), smoothed_mean_stress


def interpolate(source_fields, lon_table, cell_table, frac_table, angle_table):
    row_index = jnp.arange(ROWS, dtype=jnp.int32)
    colat_group = jnp.where(row_index < 2 * POLAR_CELL_COUNT, (row_index % POLAR_CELL_COUNT) // CT,
                            jnp.where(row_index < 2 * POLAR_CELL_COUNT + AZIMUTH_COUNT, 0, POLAR_CELL_COUNT // CT - 1))
    polar_index = (colat_group * CT + cell_table // CP).astype(jnp.int32)
    azimuth_index = (lon_table * CP + cell_table % CP).astype(jnp.int32)
    corner_first = source_fields[:, polar_index, azimuth_index]
    corner_east = source_fields[:, polar_index, azimuth_index + 1]
    corner_south = source_fields[:, polar_index + 1, azimuth_index]
    corner_last = source_fields[:, polar_index + 1, azimuth_index + 1]
    return blend_rotate(corner_first, corner_east, corner_south, corner_last, frac_table[0], frac_table[1], angle_table)


def place_border(haloed_quantity, border):
    haloed_quantity = haloed_quantity.at[:, 1:POLAR_CELL_COUNT + 1, 0].set(border[:, :POLAR_CELL_COUNT])
    haloed_quantity = haloed_quantity.at[:, 1:POLAR_CELL_COUNT + 1, AZIMUTH_COUNT + 1].set(border[:, POLAR_CELL_COUNT:2 * POLAR_CELL_COUNT])
    haloed_quantity = haloed_quantity.at[:, 0, 1:AZIMUTH_COUNT + 1].set(border[:, 2 * POLAR_CELL_COUNT:2 * POLAR_CELL_COUNT + AZIMUTH_COUNT])
    haloed_quantity = haloed_quantity.at[:, POLAR_CELL_COUNT + 1, 1:AZIMUTH_COUNT + 1].set(border[:, 2 * POLAR_CELL_COUNT + AZIMUTH_COUNT:])
    return haloed_quantity


def reference(flow_vector, mean_stress, shear_resistance, thermal_anomaly, source_azimuth_portion, source_first_slot, source_bilinear_weights, source_frame_rotation):
    colatitude_spacing = 0.5 * math.pi / POLAR_CELL_COUNT
    longitude_spacing = 1.5 * math.pi / AZIMUTH_COUNT
    colatitude_value = 0.25 * math.pi + (jnp.arange(POLAR_CELL_COUNT + 2, dtype=jnp.float32) - 0.5) * colatitude_spacing
    inner_shell_radius = INNER_RATIO * DEPTH_LEVELS
    fields_now = [jnp.concatenate([flow_vector[patch_identifier], mean_stress[patch_identifier][None], shear_resistance[patch_identifier][None]], axis=0)
                  for patch_identifier in range(2)]
    haloed_resistance_sequence = [None, None]
    for sweep_index in range(SWEEPS):
        borders = [interpolate(fields_now[1 - patch_identifier], source_azimuth_portion[1 - patch_identifier], source_first_slot[1 - patch_identifier],
                               source_bilinear_weights[1 - patch_identifier], source_frame_rotation[1 - patch_identifier]) for patch_identifier in range(2)]
        next_fields = []
        for patch_identifier in range(2):
            haloed_quantity = jnp.pad(fields_now[patch_identifier], ((0, 0), (1, 1), (1, 1), (0, 0)))
            haloed_quantity = place_border(haloed_quantity, borders[patch_identifier])
            if sweep_index == 0:
                haloed_resistance_sequence[patch_identifier] = haloed_quantity[4]
            smoothed_flow_vector, smoothed_mean_stress = weighted_smoothing_pass(haloed_quantity[:3], haloed_quantity[3], haloed_resistance_sequence[patch_identifier], thermal_anomaly[patch_identifier],
                                                     colatitude_value, inner_shell_radius, colatitude_spacing, longitude_spacing)
            next_fields.append(jnp.concatenate([smoothed_flow_vector, smoothed_mean_stress[None]], axis=0))
        fields_now = next_fields
    velocity_out = jnp.stack([fields_now[0][:3], fields_now[1][:3]], axis=0)
    pressure_out = jnp.stack([fields_now[0][3], fields_now[1][3]], axis=0)
    return velocity_out, pressure_out
```

```python
import functools
import math

import jax
import jax.numpy as jnp
import numpy as np
from jax import lax
from jax.experimental import pallas as pl
from jax.experimental.pallas import tpu as pltpu
from jax.sharding import PartitionSpec as P

OMEGA_VELOCITY = 0.8
OMEGA_PRESSURE = 0.1
INNER_RATIO = 11.0 / 9.0
LEFT = 8
HIGHEST = lax.Precision.HIGHEST
SCALARS = 8


def row_constants(tc, ac, lon, colat):
    pt, at = tc * colat, ac * lon
    rows = np.arange(2 * pt + 2 * at)
    side = rows < 2 * pt
    off = rows - 2 * pt
    group = np.where(side, rows % pt // tc, np.where(off < at, 0, colat - 1))
    target = np.where(rows < pt, 0, np.where(side, lon - 1, off % at // ac))
    place = np.where(side, rows % tc, tc + off % at % ac)
    return np.stack([target, group, place + 1]).astype(np.int32)


def polar_constants(tc, ac, lon, colat):
    pt, at = tc * colat, ac * lon
    dth, dph = 0.5 * math.pi / pt, 1.5 * math.pi / at
    th = 0.25 * math.pi + (np.arange(pt, dtype=np.float64) + 0.5) * dth
    s = np.sin(th)
    table = np.zeros((pt, SCALARS))
    table[:, 0] = 0.5 * np.sin(th - 0.5 * dth) / s / dth**2
    table[:, 1] = 0.5 * np.sin(th + 0.5 * dth) / s / dth**2
    table[:, 2] = 0.5 / (s * dph) ** 2
    table[:, 3] = 0.5 / dth
    table[:, 4] = 0.5 / (s * dph)
    table[:, 5] = np.sin(th - dth) / (2 * dth * s)
    table[:, 6] = np.sin(th + dth) / (2 * dth * s)
    return table.reshape(-1).astype(np.float32)


def kernel(
    dims,
    polar_ref,
    const_ref,
    portion_ref,
    slot_ref,
    weight_ref,
    angle_ref,
    flow_hbm,
    pres_hbm,
    visc_hbm,
    heat_hbm,
    vel_out,
    pres_out,
    pad1,
    pad2,
    heat,
    coef,
    lon_send,
    lon_recv,
    send1,
    send2,
    recv1,
    recv2,
    in_sem,
    lon_ssem,
    lon_rsem,
    col_ssem,
    col_rsem,
    pan_ssem,
    pan_rsem,
):
    tc, ac, nk, lon, colat, slots, pack = dims
    rows = const_ref.shape[1]
    cells = tc * ac
    ghosts = tc + ac
    packed = 8 * lon
    p = lax.axis_index("panel")
    l = lax.axis_index("lon")
    c = lax.axis_index("colat")
    other = 1 - p
    inner = pl.ds(LEFT, ac)
    pads, sends, recvs, counts = (pad1, pad2), (send1, send2), (recv1, recv2), (5, 4)

    local = [
        pltpu.make_async_copy(flow_hbm.at[0], pad1.at[0:3, 1 : tc + 1, inner, :], in_sem.at[0]),
        pltpu.make_async_copy(pres_hbm.at[0], pad1.at[3, 1 : tc + 1, inner, :], in_sem.at[1]),
        pltpu.make_async_copy(visc_hbm.at[0], pad1.at[4, 1 : tc + 1, inner, :], in_sem.at[2]),
        pltpu.make_async_copy(heat_hbm.at[0], heat, in_sem.at[3]),
    ]
    for copy in local:
        copy.start()

    barrier = pltpu.get_barrier_semaphore()

    def greet(**where):
        pl.semaphore_signal(
            barrier, inc=1, device_id=where, device_id_type=pl.DeviceIdType.MESH
        )

    def greet_panel(k, carry):
        greet(panel=other, lon=lax.rem(l + k, lon))
        return carry

    lax.fori_loop(0, lon, greet_panel, 0)
    has = {"w": l > 0, "e": l < lon - 1, "n": c > 0, "s": c < colat - 1}
    pl.when(has["w"])(lambda: greet(lon=l - 1))
    pl.when(has["e"])(lambda: greet(lon=l + 1))
    pl.when(has["n"])(lambda: greet(colat=c - 1))
    pl.when(has["s"])(lambda: greet(colat=c + 1))

    target = const_ref[0:1, :]
    serving = (portion_ref[...] == l) & (const_ref[1:2, :] == c)
    wanted = jnp.where(serving, target, -1)
    lon_iota = lax.broadcasted_iota(jnp.int32, (lon, rows), 0)
    member = wanted == lon_iota
    member_f = member.astype(jnp.float32)
    before = (
        lax.broadcasted_iota(jnp.int32, (rows, rows), 0)
        < lax.broadcasted_iota(jnp.int32, (rows, rows), 1)
    ).astype(jnp.float32)
    running = jnp.dot(
        member_f.astype(jnp.bfloat16),
        before.astype(jnp.bfloat16),
        preferred_element_type=jnp.float32,
    )
    rank = jnp.sum(jnp.where(member, running, 0.0), axis=0, keepdims=True)
    key = jnp.where(serving, target.astype(jnp.float32) * slots + rank, -1.0)
    key = jnp.where(rank < slots, key, -1.0)
    line = lax.broadcasted_iota(jnp.int32, (packed, rows), 0)
    line_key = (line >> 3) * slots + (line & (slots - 1))
    chosen = key == line_key.astype(jnp.float32)

    def picked(values):
        return jnp.sum(jnp.where(chosen, values, 0.0), axis=1, keepdims=True)

    angle = angle_ref[...]
    donor = picked(slot_ref[...].astype(jnp.float32))
    frac_t = picked(weight_ref[0, 0:1, :])
    frac_j = picked(weight_ref[0, 1:2, :])
    cosine = picked(jnp.cos(angle))
    sine = picked(jnp.sin(angle))
    ghost_id = picked(const_ref[2:3, :].astype(jnp.float32))
    used = jnp.where(ghost_id > 0.5, 1.0, 0.0)
    step = lax.broadcasted_iota(jnp.int32, (packed, cells), 1).astype(jnp.float32) - donor
    keep_t = (1.0 - frac_t) * used
    lean_t = frac_t * used
    blend = jnp.where(step == 0.0, keep_t * (1.0 - frac_j), 0.0)
    blend = jnp.where(step == 1.0, keep_t * frac_j, blend)
    blend = jnp.where(step == float(ac), lean_t * (1.0 - frac_j), blend)
    blend = jnp.where(step == float(ac + 1), lean_t * frac_j, blend)
    block_of = (
        (lax.broadcasted_iota(jnp.int32, (packed, nk), 0) & 7) >> (slots.bit_length() - 1)
    )

    def lon_copy(sweep, side):
        n = counts[sweep]
        return pltpu.make_async_remote_copy(
            src_ref=lon_send.at[sweep, side, 0:n],
            dst_ref=lon_recv.at[sweep, side, 0:n],
            send_sem=lon_ssem.at[sweep, side],
            recv_sem=lon_rsem.at[sweep, side],
            device_id={"lon": jnp.maximum(l - 1, 0) if side == 0 else jnp.minimum(l + 1, lon - 1)},
            device_id_type=pl.DeviceIdType.MESH,
        )

    def colat_copy(sweep, side):
        pad = pads[sweep]
        from_row, to_row = (1, tc + 1) if side == 0 else (tc, 0)
        return pltpu.make_async_remote_copy(
            src_ref=pad.at[:, from_row, inner, :],
            dst_ref=pad.at[:, to_row, inner, :],
            send_sem=col_ssem.at[sweep, side],
            recv_sem=col_rsem.at[sweep, side],
            device_id={"colat": jnp.maximum(c - 1, 0) if side == 0 else jnp.minimum(c + 1, colat - 1)},
            device_id_type=pl.DeviceIdType.MESH,
        )

    def panel_copy(sweep, to, slot):
        return pltpu.make_async_remote_copy(
            src_ref=sends[sweep].at[to],
            dst_ref=recvs[sweep].at[slot],
            send_sem=pan_ssem.at[sweep, to],
            recv_sem=pan_rsem.at[sweep, slot],
            device_id={"panel": other, "lon": to},
            device_id_type=pl.DeviceIdType.MESH,
        )

    def stage_lon(sweep):
        pad = pads[sweep]
        for f in range(counts[sweep]):
            lon_send[sweep, 0, f] = pad[f, 1 : tc + 1, LEFT, :]
            lon_send[sweep, 1, f] = pad[f, 1 : tc + 1, LEFT + ac - 1, :]

    def start_halos(sweep):
        pl.when(has["n"])(lambda: colat_copy(sweep, 0).start())
        pl.when(has["s"])(lambda: colat_copy(sweep, 1).start())
        pl.when(has["w"])(lambda: lon_copy(sweep, 0).start())
        pl.when(has["e"])(lambda: lon_copy(sweep, 1).start())

    def gather(sweep):
        pad, send, n = pads[sweep], sends[sweep], counts[sweep]
        fields = [
            jnp.dot(
                blend,
                pad[f, 1 : tc + 1, inner, :].reshape(cells, nk),
                precision=HIGHEST,
                preferred_element_type=jnp.float32,
            )
            for f in range(n)
        ]
        polar, azimuth = fields[1], fields[2]
        fields[1] = cosine * polar + sine * azimuth
        fields[2] = cosine * azimuth - sine * polar
        if sweep == 0:
            fields.append(jnp.broadcast_to(ghost_id, (packed, nk)))
        for m in range(send.shape[1]):
            tile = jnp.zeros((packed, nk), jnp.float32)
            for h in range(pack):
                if m * pack + h < len(fields):
                    tile = jnp.where(block_of == h, fields[m * pack + h], tile)
            send[:, m] = tile.reshape(lon, 8, nk)

    def start_panel(sweep):
        def one(k, carry):
            panel_copy(sweep, lax.rem(l + k, lon), l).start()
            return carry

        lax.fori_loop(0, lon, one, 0)

    def wait_all(sweep):
        pl.when(has["e"])(lambda: lon_copy(sweep, 0).wait_recv())
        pl.when(has["w"])(lambda: lon_copy(sweep, 1).wait_recv())
        pl.when(has["s"])(lambda: colat_copy(sweep, 0).wait_recv())
        pl.when(has["n"])(lambda: colat_copy(sweep, 1).wait_recv())

        def one(k, carry):
            panel_copy(sweep, k, k).wait_recv()
            return carry

        lax.fori_loop(0, lon, one, 0)

    def wait_sent(sweep):
        pl.when(has["n"])(lambda: colat_copy(sweep, 0).wait_send())
        pl.when(has["s"])(lambda: colat_copy(sweep, 1).wait_send())
        pl.when(has["w"])(lambda: lon_copy(sweep, 0).wait_send())
        pl.when(has["e"])(lambda: lon_copy(sweep, 1).wait_send())

        def one(k, carry):
            panel_copy(sweep, k, l).wait_send()
            return carry

        lax.fori_loop(0, lon, one, 0)

    def placing():
        m, h = 5 // pack, 5 % pack
        tile = recv1[:, m].reshape(packed, nk)
        ids = jnp.where(block_of == h, tile, 0.0).reshape(lon, 8, nk)
        total = ids
        for turn in range(1, pack):
            total = total + pltpu.roll(ids, turn * slots, 1)
        total = total.reshape(packed, nk)
        blocks = []
        for h in range(pack):
            place = lax.broadcasted_iota(jnp.int32, (packed, ghosts), 1).astype(jnp.float32) + 1.0
            hit = (total[:, :ghosts] == place) & (block_of[:, :ghosts] == h)
            blocks.append(jnp.where(hit, 1.0, 0.0))
        return jnp.concatenate(blocks, axis=1)

    def assemble(sweep, where_to):
        pad, recv, n = pads[sweep], recvs[sweep], counts[sweep]
        for m in range(recv.shape[1]):
            if m * pack >= n:
                continue
            placed = lax.dot_general(
                where_to,
                recv[:, m].reshape(packed, nk),
                (((0,), (0,)), ((), ())),
                precision=HIGHEST,
                preferred_element_type=jnp.float32,
            )
            for h in range(pack):
                f = m * pack + h
                if f >= n:
                    continue
                mine = placed[h * ghosts : (h + 1) * ghosts]
                side, band = mine[:tc], mine[tc:]
                pad[f, 1 : tc + 1, LEFT - 1, :] = jnp.where(has["w"], lon_recv[sweep, 1, f], side)
                pad[f, 1 : tc + 1, LEFT + ac, :] = jnp.where(has["e"], lon_recv[sweep, 0, f], side)

                @pl.when(c == 0)
                def _():
                    pad[f, 0, inner, :] = band

                @pl.when(c == colat - 1)
                def _():
                    pad[f, tc + 1, inner, :] = band

    lane = lax.broadcasted_iota(jnp.int32, (1, nk), 1)
    radius = INNER_RATIO * nk + lane.astype(jnp.float32) + 0.5
    inv = 1.0 / radius
    inv2 = inv * inv
    top, bottom = lane == nk - 1, lane == 0
    up_geo = 0.5 * ((radius + 0.5) * inv) ** 2
    down_geo = 0.5 * ((radius - 0.5) * inv) ** 2
    grad_up = jnp.where(top, 0.0, 0.5)
    grad_down = jnp.where(bottom, 0.0, 0.5)
    div_up = jnp.where(top, 0.0, 0.5 * ((radius + 1.0) * inv) ** 2)
    div_down = jnp.where(bottom, 0.0, 0.5 * ((radius - 1.0) * inv) ** 2)

    def above(x):
        return pltpu.roll(x, nk - 1, 1)

    def below(x):
        return pltpu.roll(x, 1, 1)

    def smooth(sweep):
        pad = pads[sweep]

        def row(t, carry):
            scalar = lambda i: polar_ref[(c * tc + t) * SCALARS + i]

            def near(f):
                return (
                    pad[f, t + 1, inner, :],
                    pad[f, t, inner, :],
                    pad[f, t + 2, inner, :],
                    pad[f, t + 1, pl.ds(LEFT - 1, ac), :],
                    pad[f, t + 1, pl.ds(LEFT + 1, ac), :],
                )

            if sweep == 0:
                e, en, es, ew, ee = near(4)
                e_up = jnp.where(top, e, above(e))
                e_dn = jnp.where(bottom, e, below(e))
                a_up = (e + e_up) * up_geo
                a_dn = (e + e_dn) * down_geo
                a_n = (e + en) * (scalar(0) * inv2)
                a_s = (e + es) * (scalar(1) * inv2)
                h2 = scalar(2) * inv2
                a_w = (e + ew) * h2
                a_e = (e + ee) * h2
                d = OMEGA_VELOCITY / (a_up + a_dn + a_n + a_s + a_w + a_e)
                b_up = jnp.where(top, 0.0, a_up * d)
                b_dn = jnp.where(bottom, 0.0, a_dn * d)
                b_n, b_s, b_w, b_e = a_n * d, a_s * d, a_w * d, a_e * d
                for i, b in enumerate((b_up, b_dn, b_n, b_s, b_w, b_e, d)):
                    coef[i, t] = b
            else:
                b_up, b_dn, b_n, b_s, b_w, b_e, d = [coef[i, t] for i in range(7)]
                e = pad1[4, t + 1, inner, :]
            pc, pn, ps, pw, pe = near(3)
            az = scalar(4) * inv
            forcing = (
                heat[t] - (grad_up * above(pc) - grad_down * below(pc)),
                (pn - ps) * (scalar(3) * inv),
                (pw - pe) * az,
            )
            new = []
            div = None
            for f in range(3):
                w, wn, ws, ww, we = near(f)
                wu, wd = above(w), below(w)
                total = b_up * wu + b_dn * wd + b_n * wn + b_s * ws + b_w * ww + b_e * we
                new.append((1.0 - OMEGA_VELOCITY) * w + (total + d * forcing[f]))
                if f == 0:
                    div = div_up * wu - div_down * wd
                elif f == 1:
                    div = div + (scalar(6) * ws - scalar(5) * wn) * inv
                else:
                    div = div + (we - ww) * az
            new.append(pc - OMEGA_PRESSURE * e * div)
            if sweep == 0:
                for f in range(4):
                    pad2[f, t + 1, inner, :] = new[f]
            else:
                for f in range(3):
                    vel_out[0, f, t] = new[f]
                pres_out[0, t] = new[3]
            return carry

        lax.fori_loop(0, tc, row, 0)

    greeted = lon + sum(has[side].astype(jnp.int32) for side in "wens")
    for copy in local:
        copy.wait()
    gather(0)
    stage_lon(0)
    pl.semaphore_wait(barrier, greeted)
    start_panel(0)
    start_halos(0)
    wait_all(0)
    where_to = placing()
    assemble(0, where_to)
    smooth(0)
    stage_lon(1)
    start_halos(1)
    gather(1)
    start_panel(1)
    wait_all(1)
    assemble(1, where_to)
    smooth(1)
    wait_sent(0)
    wait_sent(1)


def body(lon, colat, flow, pres, visc, heat, portion, slot, weights, angle):
    tc, ac, nk = flow.shape[2:]
    rows = portion.shape[1]
    pair_rows = (tc + ac + lon - 1) // lon
    slots = 1
    while slots < pair_rows:
        slots *= 2
    pack = 8 // slots
    tiles1, tiles2 = -(-6 // pack), -(-4 // pack)
    f32 = jnp.float32
    vmem = pl.BlockSpec(memory_space=pltpu.VMEM)
    hbm = pl.BlockSpec(memory_space=pl.ANY)
    smem = pl.BlockSpec(memory_space=pltpu.SMEM)
    wide = LEFT + ac + 8
    return pl.pallas_call(
        functools.partial(kernel, (tc, ac, nk, lon, colat, slots, pack)),
        out_shape=(jax.ShapeDtypeStruct(flow.shape, f32), jax.ShapeDtypeStruct(pres.shape, f32)),
        in_specs=[smem] + [vmem] * 5 + [hbm] * 4,
        out_specs=(vmem, vmem),
        scratch_shapes=[
            pltpu.VMEM((5, tc + 2, wide, nk), f32),
            pltpu.VMEM((4, tc + 2, wide, nk), f32),
            pltpu.VMEM((tc, ac, nk), f32),
            pltpu.VMEM((7, tc, ac, nk), f32),
            pltpu.VMEM((2, 2, 5, tc, nk), f32),
            pltpu.VMEM((2, 2, 5, tc, nk), f32),
            pltpu.VMEM((lon, tiles1, 8, nk), f32),
            pltpu.VMEM((lon, tiles2, 8, nk), f32),
            pltpu.VMEM((lon, tiles1, 8, nk), f32),
            pltpu.VMEM((lon, tiles2, 8, nk), f32),
            pltpu.SemaphoreType.DMA((4,)),
            pltpu.SemaphoreType.DMA((2, 2)),
            pltpu.SemaphoreType.DMA((2, 2)),
            pltpu.SemaphoreType.DMA((2, 2)),
            pltpu.SemaphoreType.DMA((2, 2)),
            pltpu.SemaphoreType.DMA((2, lon)),
            pltpu.SemaphoreType.DMA((2, lon)),
        ],
        compiler_params=pltpu.CompilerParams(
            collective_id=0, has_side_effects=True, vmem_limit_bytes=48 * 1024 * 1024
        ),
    )(
        jnp.asarray(polar_constants(tc, ac, lon, colat)),
        jnp.asarray(row_constants(tc, ac, lon, colat)),
        portion,
        slot,
        weights,
        angle,
        flow,
        pres,
        visc,
        heat,
    )


def solution(mesh):
    return jax.shard_map(
        functools.partial(body, mesh.shape["lon"], mesh.shape["colat"]),
        mesh=mesh,
        in_specs=(
            P("panel", None, "colat", "lon", None),
            P("panel", "colat", "lon", None),
            P("panel", "colat", "lon", None),
            P("panel", "colat", "lon", None),
            P("panel", None),
            P("panel", None),
            P("panel", None, None),
            P("panel", None),
        ),
        out_specs=(P("panel", None, "colat", "lon", None), P("panel", "colat", "lon", None)),
        check_vma=False,
    )
```

```python
import functools
import math

import jax
import jax.numpy as jnp
import numpy as np
from jax import lax
from jax.experimental import pallas as pl
from jax.experimental.pallas import tpu as pltpu
from jax.sharding import PartitionSpec as P

OMEGA_VELOCITY = 0.8
OMEGA_PRESSURE = 0.1
INNER_RATIO = 11.0 / 9.0
LEFT = 8
HIGHEST = lax.Precision.HIGHEST
SCALARS = 8


def row_constants(tc, ac, lon, colat):
    pt, at = tc * colat, ac * lon
    rows = np.arange(2 * pt + 2 * at)
    side = rows < 2 * pt
    off = rows - 2 * pt
    group = np.where(side, rows % pt // tc, np.where(off < at, 0, colat - 1))
    target = np.where(rows < pt, 0, np.where(side, lon - 1, off % at // ac))
    place = np.where(side, rows % tc, tc + off % at % ac)
    return np.stack([target, group, place + 1]).astype(np.int32)


def polar_constants(tc, ac, lon, colat):
    pt, at = tc * colat, ac * lon
    dth, dph = 0.5 * math.pi / pt, 1.5 * math.pi / at
    th = 0.25 * math.pi + (np.arange(pt, dtype=np.float64) + 0.5) * dth
    s = np.sin(th)
    table = np.zeros((pt, SCALARS))
    table[:, 0] = 0.5 * np.sin(th - 0.5 * dth) / s / dth**2
    table[:, 1] = 0.5 * np.sin(th + 0.5 * dth) / s / dth**2
    table[:, 2] = 0.5 / (s * dph) ** 2
    table[:, 3] = 0.5 / dth
    table[:, 4] = 0.5 / (s * dph)
    table[:, 5] = np.sin(th - dth) / (2 * dth * s)
    table[:, 6] = np.sin(th + dth) / (2 * dth * s)
    return table.reshape(-1).astype(np.float32)


def above(x):
    return pltpu.roll(x, x.shape[1] - 1, 1)


def below(x):
    return pltpu.roll(x, 1, 1)


def radial(nk):
    lane = lax.broadcasted_iota(jnp.int32, (1, nk), 1)
    radius = INNER_RATIO * nk + lane.astype(jnp.float32) + 0.5
    inv = 1.0 / radius
    top, bottom = lane == nk - 1, lane == 0
    return {
        "inv": inv,
        "top": top,
        "bottom": bottom,
        "up_geo": 0.5 * ((radius + 0.5) * inv) ** 2,
        "down_geo": 0.5 * ((radius - 0.5) * inv) ** 2,
        "grad_up": jnp.where(top, 0.0, 0.5),
        "grad_down": jnp.where(bottom, 0.0, 0.5),
        "div_up": jnp.where(top, 0.0, 0.5 * ((radius + 1.0) * inv) ** 2),
        "div_down": jnp.where(bottom, 0.0, 0.5 * ((radius - 1.0) * inv) ** 2),
    }


def smoothed(pad, t, ac, lane, factors, steps):
    b_up, b_dn, b_n, b_s, b_w, b_e, d, e, heat = factors
    polar, azimuth, div_n, div_s = steps
    inner = pl.ds(LEFT, ac)

    def near(f):
        return (
            pad[f, t + 1, inner, :],
            pad[f, t, inner, :],
            pad[f, t + 2, inner, :],
            pad[f, t + 1, pl.ds(LEFT - 1, ac), :],
            pad[f, t + 1, pl.ds(LEFT + 1, ac), :],
        )

    pc, pn, ps, pw, pe = near(3)
    forcing = (
        heat - d * (lane["grad_up"] * above(pc) - lane["grad_down"] * below(pc)),
        d * ((pn - ps) * polar),
        d * ((pw - pe) * azimuth),
    )
    new, div = [], None
    for f in range(3):
        w, wn, ws, ww, we = near(f)
        wu, wd = above(w), below(w)
        total = b_up * wu + b_dn * wd + b_n * wn + b_s * ws + b_w * ww + b_e * we
        new.append((1.0 - OMEGA_VELOCITY) * w + (total + forcing[f]))
        if f == 0:
            div = lane["div_up"] * wu - lane["div_down"] * wd
        elif f == 1:
            div = div + (div_s * ws - div_n * wn)
        else:
            div = div + (we - ww) * azimuth
    new.append(pc - e * div)
    return new


def last_kernel(dims, pad, coef, geo, vel_hbm, pres_hbm, vel, pres, sem):
    tc, ac, nk = dims
    lane = radial(nk)
    parts = 2 if tc % 2 == 0 else 1
    size = tc // parts

    def row(t, carry):
        factors = [coef[i, t] for i in range(9)]
        steps = [geo[i, t, 0:1, :] for i in range(4)]
        new = smoothed(pad, t, ac, lane, factors, steps)
        for f in range(3):
            vel[f, t] = new[f]
        pres[t] = new[3]
        return carry

    copies = []
    for part in range(parts):
        lo, hi = part * size, (part + 1) * size
        lax.fori_loop(lo, hi, row, 0)
        copies += [
            pltpu.make_async_copy(vel.at[:, lo:hi], vel_hbm.at[0, :, lo:hi], sem.at[part, 0]),
            pltpu.make_async_copy(pres.at[lo:hi], pres_hbm.at[0, lo:hi], sem.at[part, 1]),
        ]
        for copy in copies[-2:]:
            copy.start()
    for copy in copies:
        copy.wait()


def kernel(
    dims,
    polar_hbm,
    const_hbm,
    portion_hbm,
    slot_hbm,
    weight_hbm,
    angle_hbm,
    flow_hbm,
    pres_hbm,
    visc_hbm,
    heat_hbm,
    pad2,
    coef,
    geo,
    pad1,
    heat,
    polar_ref,
    const_ref,
    portion_ref,
    slot_ref,
    weight_ref,
    angle_ref,
    lon_send,
    lon_recv,
    send1,
    send2,
    recv1,
    recv2,
    in_sem,
    lon_ssem,
    lon_rsem,
    col_ssem,
    col_rsem,
    pan_ssem,
    pan_rsem,
):
    tc, ac, nk, lon, colat, slots, pack = dims
    rows = const_ref.shape[1]
    cells = tc * ac
    ghosts = tc + ac
    packed = 8 * lon
    p = lax.axis_index("panel")
    l = lax.axis_index("lon")
    c = lax.axis_index("colat")
    other = 1 - p
    inner = pl.ds(LEFT, ac)
    pads, sends, recvs, counts = (pad1, pad2), (send1, send2), (recv1, recv2), (5, 4)

    local = [
        pltpu.make_async_copy(flow_hbm.at[0], pad1.at[0:3, 1 : tc + 1, inner, :], in_sem.at[0]),
        pltpu.make_async_copy(pres_hbm.at[0], pad1.at[3, 1 : tc + 1, inner, :], in_sem.at[1]),
        pltpu.make_async_copy(visc_hbm.at[0], pad1.at[4, 1 : tc + 1, inner, :], in_sem.at[2]),
        pltpu.make_async_copy(heat_hbm.at[0], heat, in_sem.at[3]),
        pltpu.make_async_copy(polar_hbm, polar_ref, in_sem.at[4]),
    ]
    tables = [
        pltpu.make_async_copy(const_hbm, const_ref, in_sem.at[5]),
        pltpu.make_async_copy(portion_hbm, portion_ref, in_sem.at[6]),
        pltpu.make_async_copy(slot_hbm, slot_ref, in_sem.at[7]),
        pltpu.make_async_copy(weight_hbm, weight_ref, in_sem.at[8]),
        pltpu.make_async_copy(angle_hbm, angle_ref, in_sem.at[9]),
    ]
    for copy in tables + local:
        copy.start()

    barrier = pltpu.get_barrier_semaphore()

    def greet(**where):
        pl.semaphore_signal(
            barrier, inc=1, device_id=where, device_id_type=pl.DeviceIdType.MESH
        )

    def greet_panel(k, carry):
        greet(panel=other, lon=lax.rem(l + k, lon))
        return carry

    lax.fori_loop(0, lon, greet_panel, 0)
    has = {"w": l > 0, "e": l < lon - 1, "n": c > 0, "s": c < colat - 1}
    pl.when(has["w"])(lambda: greet(lon=l - 1))
    pl.when(has["e"])(lambda: greet(lon=l + 1))
    pl.when(has["n"])(lambda: greet(colat=c - 1))
    pl.when(has["s"])(lambda: greet(colat=c + 1))

    for copy in tables:
        copy.wait()

    target = const_ref[0:1, :]
    serving = (portion_ref[...] == l) & (const_ref[1:2, :] == c)
    wanted = jnp.where(serving, target, -1)
    lon_iota = lax.broadcasted_iota(jnp.int32, (lon, rows), 0)
    member = wanted == lon_iota
    member_f = member.astype(jnp.float32)
    before = (
        lax.broadcasted_iota(jnp.int32, (rows, rows), 0)
        < lax.broadcasted_iota(jnp.int32, (rows, rows), 1)
    ).astype(jnp.float32)
    running = jnp.dot(
        member_f.astype(jnp.bfloat16),
        before.astype(jnp.bfloat16),
        preferred_element_type=jnp.float32,
    )
    rank = jnp.sum(jnp.where(member, running, 0.0), axis=0, keepdims=True)
    key = jnp.where(serving, target.astype(jnp.float32) * slots + rank, -1.0)
    key = jnp.where(rank < slots, key, -1.0)
    line = lax.broadcasted_iota(jnp.int32, (packed, rows), 0)
    line_key = (line >> 3) * slots + (line & (slots - 1))
    chosen = key == line_key.astype(jnp.float32)

    def picked(values):
        return jnp.sum(jnp.where(chosen, values, 0.0), axis=1, keepdims=True)

    angle = angle_ref[...]
    donor = picked(slot_ref[...].astype(jnp.float32))
    frac_t = picked(weight_ref[0, 0:1, :])
    frac_j = picked(weight_ref[0, 1:2, :])
    cosine = picked(jnp.cos(angle))
    sine = picked(jnp.sin(angle))
    ghost_id = picked(const_ref[2:3, :].astype(jnp.float32))
    used = jnp.where(ghost_id > 0.5, 1.0, 0.0)
    step = lax.broadcasted_iota(jnp.int32, (packed, cells), 1).astype(jnp.float32) - donor
    keep_t = (1.0 - frac_t) * used
    lean_t = frac_t * used
    blend = jnp.where(step == 0.0, keep_t * (1.0 - frac_j), 0.0)
    blend = jnp.where(step == 1.0, keep_t * frac_j, blend)
    blend = jnp.where(step == float(ac), lean_t * (1.0 - frac_j), blend)
    blend = jnp.where(step == float(ac + 1), lean_t * frac_j, blend)
    block_of = (
        (lax.broadcasted_iota(jnp.int32, (packed, nk), 0) & 7) >> (slots.bit_length() - 1)
    )

    def lon_copy(sweep, side):
        n = counts[sweep]
        return pltpu.make_async_remote_copy(
            src_ref=lon_send.at[sweep, side, 0:n],
            dst_ref=lon_recv.at[sweep, side, 0:n],
            send_sem=lon_ssem.at[sweep, side],
            recv_sem=lon_rsem.at[sweep, side],
            device_id={"lon": jnp.maximum(l - 1, 0) if side == 0 else jnp.minimum(l + 1, lon - 1)},
            device_id_type=pl.DeviceIdType.MESH,
        )

    def colat_copy(sweep, side):
        pad = pads[sweep]
        from_row, to_row = (1, tc + 1) if side == 0 else (tc, 0)
        return pltpu.make_async_remote_copy(
            src_ref=pad.at[:, from_row, inner, :],
            dst_ref=pad.at[:, to_row, inner, :],
            send_sem=col_ssem.at[sweep, side],
            recv_sem=col_rsem.at[sweep, side],
            device_id={"colat": jnp.maximum(c - 1, 0) if side == 0 else jnp.minimum(c + 1, colat - 1)},
            device_id_type=pl.DeviceIdType.MESH,
        )

    def panel_copy(sweep, to, slot):
        return pltpu.make_async_remote_copy(
            src_ref=sends[sweep].at[to],
            dst_ref=recvs[sweep].at[slot],
            send_sem=pan_ssem.at[sweep, to],
            recv_sem=pan_rsem.at[sweep, slot],
            device_id={"panel": other, "lon": to},
            device_id_type=pl.DeviceIdType.MESH,
        )

    def stage_lon(sweep):
        pad = pads[sweep]
        for f in range(counts[sweep]):
            lon_send[sweep, 0, f] = pad[f, 1 : tc + 1, LEFT, :]
            lon_send[sweep, 1, f] = pad[f, 1 : tc + 1, LEFT + ac - 1, :]

    def start_halos(sweep):
        pl.when(has["n"])(lambda: colat_copy(sweep, 0).start())
        pl.when(has["s"])(lambda: colat_copy(sweep, 1).start())
        pl.when(has["w"])(lambda: lon_copy(sweep, 0).start())
        pl.when(has["e"])(lambda: lon_copy(sweep, 1).start())

    def gather(sweep):
        pad, send, n = pads[sweep], sends[sweep], counts[sweep]
        fields = [
            jnp.dot(
                blend,
                pad[f, 1 : tc + 1, inner, :].reshape(cells, nk),
                precision=HIGHEST,
                preferred_element_type=jnp.float32,
            )
            for f in range(n)
        ]
        polar, azimuth = fields[1], fields[2]
        fields[1] = cosine * polar + sine * azimuth
        fields[2] = cosine * azimuth - sine * polar
        if sweep == 0:
            fields.append(jnp.broadcast_to(ghost_id, (packed, nk)))
        for m in range(send.shape[1]):
            tile = jnp.zeros((packed, nk), jnp.float32)
            for h in range(pack):
                if m * pack + h < len(fields):
                    tile = jnp.where(block_of == h, fields[m * pack + h], tile)
            send[:, m] = tile.reshape(lon, 8, nk)

    def start_panel(sweep):
        def one(k, carry):
            panel_copy(sweep, lax.rem(l + k, lon), l).start()
            return carry

        lax.fori_loop(0, lon, one, 0)

    def wait_all(sweep):
        pl.when(has["e"])(lambda: lon_copy(sweep, 0).wait_recv())
        pl.when(has["w"])(lambda: lon_copy(sweep, 1).wait_recv())
        pl.when(has["s"])(lambda: colat_copy(sweep, 0).wait_recv())
        pl.when(has["n"])(lambda: colat_copy(sweep, 1).wait_recv())

        def one(k, carry):
            panel_copy(sweep, k, k).wait_recv()
            return carry

        lax.fori_loop(0, lon, one, 0)

    def wait_sent(sweep):
        pl.when(has["n"])(lambda: colat_copy(sweep, 0).wait_send())
        pl.when(has["s"])(lambda: colat_copy(sweep, 1).wait_send())
        pl.when(has["w"])(lambda: lon_copy(sweep, 0).wait_send())
        pl.when(has["e"])(lambda: lon_copy(sweep, 1).wait_send())

        def one(k, carry):
            panel_copy(sweep, k, l).wait_send()
            return carry

        lax.fori_loop(0, lon, one, 0)

    def placing():
        m, h = 5 // pack, 5 % pack
        tile = recv1[:, m].reshape(packed, nk)
        ids = jnp.where(block_of == h, tile, 0.0).reshape(lon, 8, nk)
        total = ids
        for turn in range(1, pack):
            total = total + pltpu.roll(ids, turn * slots, 1)
        total = total.reshape(packed, nk)
        blocks = []
        for h in range(pack):
            place = lax.broadcasted_iota(jnp.int32, (packed, ghosts), 1).astype(jnp.float32) + 1.0
            hit = (total[:, :ghosts] == place) & (block_of[:, :ghosts] == h)
            blocks.append(jnp.where(hit, 1.0, 0.0))
        return jnp.concatenate(blocks, axis=1)

    def assemble(sweep, where_to):
        pad, recv, n = pads[sweep], recvs[sweep], counts[sweep]
        for m in range(recv.shape[1]):
            if m * pack >= n:
                continue
            placed = lax.dot_general(
                where_to,
                recv[:, m].reshape(packed, nk),
                (((0,), (0,)), ((), ())),
                precision=HIGHEST,
                preferred_element_type=jnp.float32,
            )
            for h in range(pack):
                f = m * pack + h
                if f >= n:
                    continue
                mine = placed[h * ghosts : (h + 1) * ghosts]
                side, band = mine[:tc], mine[tc:]
                pad[f, 1 : tc + 1, LEFT - 1, :] = jnp.where(has["w"], lon_recv[sweep, 1, f], side)
                pad[f, 1 : tc + 1, LEFT + ac, :] = jnp.where(has["e"], lon_recv[sweep, 0, f], side)

                @pl.when(c == 0)
                def _():
                    pad[f, 0, inner, :] = band

                @pl.when(c == colat - 1)
                def _():
                    pad[f, tc + 1, inner, :] = band

    lane = radial(nk)
    top, bottom, inv = lane["top"], lane["bottom"], lane["inv"]

    def first(t, carry):
        scalar = lambda i: polar_ref[(c * tc + t) * SCALARS + i]
        inv2 = inv * inv
        e = pad1[4, t + 1, inner, :]
        a_up = (e + jnp.where(top, e, above(e))) * lane["up_geo"]
        a_dn = (e + jnp.where(bottom, e, below(e))) * lane["down_geo"]
        a_n = (e + pad1[4, t, inner, :]) * (scalar(0) * inv2)
        a_s = (e + pad1[4, t + 2, inner, :]) * (scalar(1) * inv2)
        h2 = scalar(2) * inv2
        a_w = (e + pad1[4, t + 1, pl.ds(LEFT - 1, ac), :]) * h2
        a_e = (e + pad1[4, t + 1, pl.ds(LEFT + 1, ac), :]) * h2
        d = OMEGA_VELOCITY / (a_up + a_dn + a_n + a_s + a_w + a_e)
        factors = [
            jnp.where(top, 0.0, a_up * d),
            jnp.where(bottom, 0.0, a_dn * d),
            a_n * d,
            a_s * d,
            a_w * d,
            a_e * d,
            d,
            OMEGA_PRESSURE * e,
            heat[t] * d,
        ]
        steps = [scalar(i) * inv for i in (3, 4, 5, 6)]
        for i, factor in enumerate(factors):
            coef[i, t] = factor
        for i, step in enumerate(steps):
            geo[i, t] = jnp.broadcast_to(step, (8, nk))
        for f, value in enumerate(smoothed(pad1, t, ac, lane, factors, steps)):
            pad2[f, t + 1, inner, :] = value
        return carry

    greeted = lon + sum(has[side].astype(jnp.int32) for side in "wens")
    for copy in local:
        copy.wait()
    gather(0)
    stage_lon(0)
    pl.semaphore_wait(barrier, greeted)
    start_panel(0)
    start_halos(0)
    wait_all(0)
    where_to = placing()
    assemble(0, where_to)
    lax.fori_loop(0, tc, first, 0)
    stage_lon(1)
    start_halos(1)
    gather(1)
    start_panel(1)
    wait_all(1)
    assemble(1, where_to)
    wait_sent(0)
    wait_sent(1)


def body(lon, colat, flow, pres, visc, heat, portion, slot, weights, angle):
    tc, ac, nk = flow.shape[2:]
    rows = portion.shape[1]
    pair_rows = (tc + ac + lon - 1) // lon
    slots = 1
    while slots < pair_rows:
        slots *= 2
    pack = 8 // slots
    tiles1, tiles2 = -(-6 // pack), -(-4 // pack)
    f32, i32 = jnp.float32, jnp.int32
    vmem = pl.BlockSpec(memory_space=pltpu.VMEM)
    hbm = pl.BlockSpec(memory_space=pltpu.HBM)
    wide = LEFT + ac + 8
    polar = jnp.asarray(polar_constants(tc, ac, lon, colat))
    constants = jnp.asarray(row_constants(tc, ac, lon, colat))
    pad, coef, geo = pl.pallas_call(
        functools.partial(kernel, (tc, ac, nk, lon, colat, slots, pack)),
        out_shape=(
            jax.ShapeDtypeStruct((4, tc + 2, wide, nk), f32),
            jax.ShapeDtypeStruct((9, tc, ac, nk), f32),
            jax.ShapeDtypeStruct((4, tc, 8, nk), f32),
        ),
        in_specs=[hbm] * 10,
        out_specs=(vmem, vmem, vmem),
        scratch_shapes=[
            pltpu.VMEM((5, tc + 2, wide, nk), f32),
            pltpu.VMEM((tc, ac, nk), f32),
            pltpu.SMEM(polar.shape, f32),
            pltpu.VMEM(constants.shape, i32),
            pltpu.VMEM(portion.shape, i32),
            pltpu.VMEM(slot.shape, i32),
            pltpu.VMEM(weights.shape, f32),
            pltpu.VMEM(angle.shape, f32),
            pltpu.VMEM((2, 2, 5, tc, nk), f32),
            pltpu.VMEM((2, 2, 5, tc, nk), f32),
            pltpu.VMEM((lon, tiles1, 8, nk), f32),
            pltpu.VMEM((lon, tiles2, 8, nk), f32),
            pltpu.VMEM((lon, tiles1, 8, nk), f32),
            pltpu.VMEM((lon, tiles2, 8, nk), f32),
            pltpu.SemaphoreType.DMA((10,)),
            pltpu.SemaphoreType.DMA((2, 2)),
            pltpu.SemaphoreType.DMA((2, 2)),
            pltpu.SemaphoreType.DMA((2, 2)),
            pltpu.SemaphoreType.DMA((2, 2)),
            pltpu.SemaphoreType.DMA((2, lon)),
            pltpu.SemaphoreType.DMA((2, lon)),
        ],
        compiler_params=pltpu.CompilerParams(
            collective_id=0, has_side_effects=True, vmem_limit_bytes=32 * 1024 * 1024
        ),
    )(*(pltpu.with_memory_space_constraint(x, pltpu.HBM) for x in (polar, constants, portion, slot, weights, angle, flow, pres, visc, heat)))
    return pl.pallas_call(
        functools.partial(last_kernel, (tc, ac, nk)),
        out_shape=(jax.ShapeDtypeStruct(flow.shape, f32), jax.ShapeDtypeStruct(pres.shape, f32)),
        in_specs=[vmem] * 3,
        out_specs=(hbm, hbm),
        scratch_shapes=[
            pltpu.VMEM(flow.shape[1:], f32),
            pltpu.VMEM(pres.shape[1:], f32),
            pltpu.SemaphoreType.DMA((2, 2)),
        ],
        compiler_params=pltpu.CompilerParams(vmem_limit_bytes=32 * 1024 * 1024),
    )(pad, coef, geo)


def solution(mesh):
    return jax.shard_map(
        functools.partial(body, mesh.shape["lon"], mesh.shape["colat"]),
        mesh=mesh,
        in_specs=(
            P("panel", None, "colat", "lon", None),
            P("panel", "colat", "lon", None),
            P("panel", "colat", "lon", None),
            P("panel", "colat", "lon", None),
            P("panel", None),
            P("panel", None),
            P("panel", None, None),
            P("panel", None),
        ),
        out_specs=(P("panel", None, "colat", "lon", None), P("panel", "colat", "lon", None)),
        check_vma=False,
    )
```

```python
import functools
import math

import jax
import jax.numpy as jnp
import numpy as np
from jax import lax
from jax.experimental import pallas as pl
from jax.experimental.pallas import tpu as pltpu
from jax.sharding import PartitionSpec as P

OMEGA_VELOCITY = 0.8
OMEGA_PRESSURE = 0.1
INNER_RATIO = 11.0 / 9.0
LEFT = 8
HIGHEST = lax.Precision.HIGHEST
SCALARS = 8


def row_constants(tc, ac, lon, colat):
    pt, at = tc * colat, ac * lon
    rows = np.arange(2 * pt + 2 * at)
    side = rows < 2 * pt
    off = rows - 2 * pt
    group = np.where(side, rows % pt // tc, np.where(off < at, 0, colat - 1))
    target = np.where(rows < pt, 0, np.where(side, lon - 1, off % at // ac))
    place = np.where(side, rows % tc, tc + off % at % ac)
    return np.stack([target, group, place + 1]).astype(np.int32)


def polar_constants(tc, ac, lon, colat):
    pt, at = tc * colat, ac * lon
    dth, dph = 0.5 * math.pi / pt, 1.5 * math.pi / at
    th = 0.25 * math.pi + (np.arange(pt, dtype=np.float64) + 0.5) * dth
    s = np.sin(th)
    table = np.zeros((pt, SCALARS))
    table[:, 0] = 0.5 * np.sin(th - 0.5 * dth) / s / dth**2
    table[:, 1] = 0.5 * np.sin(th + 0.5 * dth) / s / dth**2
    table[:, 2] = 0.5 / (s * dph) ** 2
    table[:, 3] = 0.5 / dth
    table[:, 4] = 0.5 / (s * dph)
    table[:, 5] = np.sin(th - dth) / (2 * dth * s)
    table[:, 6] = np.sin(th + dth) / (2 * dth * s)
    return table.reshape(-1).astype(np.float32)


def above(x):
    return pltpu.roll(x, x.shape[2] - 1, 2)


def below(x):
    return pltpu.roll(x, 1, 2)


def west(j, nj):
    return pl.ds(LEFT + j - 1, nj)


def east(j, nj):
    return pl.ds(LEFT + j + 1, nj)


def radial(nk):
    lane = lax.broadcasted_iota(jnp.int32, (1, 1, nk), 2)
    radius = INNER_RATIO * nk + lane.astype(jnp.float32) + 0.5
    inv = 1.0 / radius
    top, bottom = lane == nk - 1, lane == 0
    return {
        "inv": inv,
        "top": top,
        "bottom": bottom,
        "up_geo": 0.5 * ((radius + 0.5) * inv) ** 2,
        "down_geo": 0.5 * ((radius - 0.5) * inv) ** 2,
        "grad_up": jnp.where(top, 0.0, 0.5),
        "grad_down": jnp.where(bottom, 0.0, 0.5),
        "div_up": jnp.where(top, 0.0, 0.5 * ((radius + 1.0) * inv) ** 2),
        "div_down": jnp.where(bottom, 0.0, 0.5 * ((radius - 1.0) * inv) ** 2),
    }


def smoothed(pad, t, nt, j, nj, lane, factors, steps):
    b_up, b_dn, b_n, b_s, b_w, b_e, d, e, heat = factors
    polar, azimuth, div_n, div_s = steps
    here, cols = pl.ds(t + 1, nt), pl.ds(LEFT + j, nj)

    def near(f):
        return (
            pad[f, here, cols, :],
            pad[f, pl.ds(t, nt), cols, :],
            pad[f, pl.ds(t + 2, nt), cols, :],
            pad[f, here, west(j, nj), :],
            pad[f, here, east(j, nj), :],
        )

    pc, pn, ps, pw, pe = near(3)
    forcing = (
        heat - d * (lane["grad_up"] * above(pc) - lane["grad_down"] * below(pc)),
        d * ((pn - ps) * polar),
        d * ((pw - pe) * azimuth),
    )
    new, div = [], None
    for f in range(3):
        w, wn, ws, ww, we = near(f)
        wu, wd = above(w), below(w)
        total = b_up * wu + b_dn * wd + b_n * wn + b_s * ws + b_w * ww + b_e * we
        new.append((1.0 - OMEGA_VELOCITY) * w + (total + forcing[f]))
        if f == 0:
            div = lane["div_up"] * wu - lane["div_down"] * wd
        elif f == 1:
            div = div + (div_s * ws - div_n * wn)
        else:
            div = div + (we - ww) * azimuth
    new.append(pc - e * div)
    return new


def copy_out(vel, pres, vel_hbm, pres_hbm, sem):
    copies = [pltpu.make_async_copy(vel.at[f], vel_hbm.at[0, f], sem.at[f]) for f in range(3)]
    copies.append(pltpu.make_async_copy(pres, pres_hbm.at[0], sem.at[3]))
    for copy in copies:
        copy.start()
    for copy in copies:
        copy.wait()


def kernel(
    dims,
    polar_hbm,
    const_hbm,
    portion_hbm,
    slot_hbm,
    weight_hbm,
    angle_hbm,
    flow_hbm,
    pres_hbm,
    visc_hbm,
    heat_hbm,
    vel,
    pres,
    pad2,
    coef,
    geo,
    pad1,
    heat,
    polar_ref,
    const_ref,
    portion_ref,
    slot_ref,
    weight_ref,
    angle_ref,
    lon_send,
    lon_recv,
    send1,
    send2,
    recv1,
    recv2,
    in_sem,
    lon_ssem,
    lon_rsem,
    col_ssem,
    col_rsem,
    pan_ssem,
    pan_rsem,
):
    tc, ac, nk, lon, colat, slots, pack = dims
    rows = const_ref.shape[1]
    cells = tc * ac
    ghosts = tc + ac
    packed = 8 * lon
    p = lax.axis_index("panel")
    l = lax.axis_index("lon")
    c = lax.axis_index("colat")
    other = 1 - p
    inner = pl.ds(LEFT, ac)
    pads, sends, recvs, counts = (pad1, pad2), (send1, send2), (recv1, recv2), (5, 4)

    local = [
        pltpu.make_async_copy(flow_hbm.at[0], pad1.at[0:3, 1 : tc + 1, inner, :], in_sem.at[0]),
        pltpu.make_async_copy(pres_hbm.at[0], pad1.at[3, 1 : tc + 1, inner, :], in_sem.at[1]),
        pltpu.make_async_copy(visc_hbm.at[0], pad1.at[4, 1 : tc + 1, inner, :], in_sem.at[2]),
        pltpu.make_async_copy(heat_hbm.at[0], heat, in_sem.at[3]),
        pltpu.make_async_copy(polar_hbm, polar_ref, in_sem.at[4]),
    ]
    tables = [
        pltpu.make_async_copy(const_hbm, const_ref, in_sem.at[5]),
        pltpu.make_async_copy(portion_hbm, portion_ref, in_sem.at[6]),
        pltpu.make_async_copy(slot_hbm, slot_ref, in_sem.at[7]),
        pltpu.make_async_copy(weight_hbm, weight_ref, in_sem.at[8]),
        pltpu.make_async_copy(angle_hbm, angle_ref, in_sem.at[9]),
    ]

    barrier = pltpu.get_barrier_semaphore()

    def distant(k):
        return l ^ (lon - 1 - k) if lon & (lon - 1) == 0 else lax.rem(l + k, lon)

    def greet(**where):
        pl.semaphore_signal(
            barrier, inc=1, device_id=where, device_id_type=pl.DeviceIdType.MESH
        )

    def greet_panel(k, carry):
        greet(panel=other, lon=distant(k))
        return carry

    lax.fori_loop(0, lon, greet_panel, 0)
    has = {"w": l > 0, "e": l < lon - 1, "n": c > 0, "s": c < colat - 1}
    pl.when(has["w"])(lambda: greet(lon=l - 1))
    pl.when(has["e"])(lambda: greet(lon=l + 1))
    pl.when(has["n"])(lambda: greet(colat=c - 1))
    pl.when(has["s"])(lambda: greet(colat=c + 1))

    for copy in tables + local:
        copy.start()
    for copy in tables:
        copy.wait()

    target = const_ref[0:1, :]
    serving = (portion_ref[...] == l) & (const_ref[1:2, :] == c)
    wanted = jnp.where(serving, target, -1)
    lon_iota = lax.broadcasted_iota(jnp.int32, (lon, rows), 0)
    member = wanted == lon_iota
    member_f = member.astype(jnp.float32)
    before = (
        lax.broadcasted_iota(jnp.int32, (rows, rows), 0)
        < lax.broadcasted_iota(jnp.int32, (rows, rows), 1)
    ).astype(jnp.float32)
    running = jnp.dot(
        member_f.astype(jnp.bfloat16),
        before.astype(jnp.bfloat16),
        preferred_element_type=jnp.float32,
    )
    rank = jnp.sum(jnp.where(member, running, 0.0), axis=0, keepdims=True)
    key = jnp.where(serving, target.astype(jnp.float32) * slots + rank, -1.0)
    key = jnp.where(rank < slots, key, -1.0)
    line = lax.broadcasted_iota(jnp.int32, (packed, rows), 0)
    line_key = (line >> 3) * slots + (line & (slots - 1))
    chosen = key == line_key.astype(jnp.float32)

    def picked(values):
        return jnp.sum(jnp.where(chosen, values, 0.0), axis=1, keepdims=True)

    angle = angle_ref[...]
    donor = picked(slot_ref[...].astype(jnp.float32))
    frac_t = picked(weight_ref[0, 0:1, :])
    frac_j = picked(weight_ref[0, 1:2, :])
    cosine = picked(jnp.cos(angle))
    sine = picked(jnp.sin(angle))
    ghost_id = picked(const_ref[2:3, :].astype(jnp.float32))
    used = jnp.where(ghost_id > 0.5, 1.0, 0.0)
    step = lax.broadcasted_iota(jnp.int32, (packed, cells), 1).astype(jnp.float32) - donor
    keep_t = (1.0 - frac_t) * used
    lean_t = frac_t * used
    blend = jnp.where(step == 0.0, keep_t * (1.0 - frac_j), 0.0)
    blend = jnp.where(step == 1.0, keep_t * frac_j, blend)
    blend = jnp.where(step == float(ac), lean_t * (1.0 - frac_j), blend)
    blend = jnp.where(step == float(ac + 1), lean_t * frac_j, blend)
    block_of = (
        (lax.broadcasted_iota(jnp.int32, (packed, nk), 0) & 7) >> (slots.bit_length() - 1)
    )

    def lon_copy(sweep, side):
        n = counts[sweep]
        return pltpu.make_async_remote_copy(
            src_ref=lon_send.at[sweep, side, 0:n],
            dst_ref=lon_recv.at[sweep, side, 0:n],
            send_sem=lon_ssem.at[sweep, side],
            recv_sem=lon_rsem.at[sweep, side],
            device_id={"lon": jnp.maximum(l - 1, 0) if side == 0 else jnp.minimum(l + 1, lon - 1)},
            device_id_type=pl.DeviceIdType.MESH,
        )

    def colat_copy(sweep, side):
        pad = pads[sweep]
        from_row, to_row = (1, tc + 1) if side == 0 else (tc, 0)
        return pltpu.make_async_remote_copy(
            src_ref=pad.at[:, from_row, inner, :],
            dst_ref=pad.at[:, to_row, inner, :],
            send_sem=col_ssem.at[sweep, side],
            recv_sem=col_rsem.at[sweep, side],
            device_id={"colat": jnp.maximum(c - 1, 0) if side == 0 else jnp.minimum(c + 1, colat - 1)},
            device_id_type=pl.DeviceIdType.MESH,
        )

    def panel_copy(sweep, to, slot):
        return pltpu.make_async_remote_copy(
            src_ref=sends[sweep].at[to],
            dst_ref=recvs[sweep].at[slot],
            send_sem=pan_ssem.at[sweep, to],
            recv_sem=pan_rsem.at[sweep, slot],
            device_id={"panel": other, "lon": to},
            device_id_type=pl.DeviceIdType.MESH,
        )

    def stage_lon(sweep):
        pad = pads[sweep]
        for f in range(counts[sweep]):
            lon_send[sweep, 0, f] = pad[f, 1 : tc + 1, LEFT, :]
            lon_send[sweep, 1, f] = pad[f, 1 : tc + 1, LEFT + ac - 1, :]

    def start_halos(sweep):
        pl.when(has["n"])(lambda: colat_copy(sweep, 0).start())
        pl.when(has["s"])(lambda: colat_copy(sweep, 1).start())
        pl.when(has["w"])(lambda: lon_copy(sweep, 0).start())
        pl.when(has["e"])(lambda: lon_copy(sweep, 1).start())

    def gather(sweep):
        pad, send, n = pads[sweep], sends[sweep], counts[sweep]
        fields = [
            jnp.dot(
                blend,
                pad[f, 1 : tc + 1, inner, :].reshape(cells, nk),
                precision=HIGHEST,
                preferred_element_type=jnp.float32,
            )
            for f in range(n)
        ]
        polar, azimuth = fields[1], fields[2]
        fields[1] = cosine * polar + sine * azimuth
        fields[2] = cosine * azimuth - sine * polar
        if sweep == 0:
            fields.append(jnp.broadcast_to(ghost_id, (packed, nk)))
        for m in range(send.shape[1]):
            tile = jnp.zeros((packed, nk), jnp.float32)
            for h in range(pack):
                if m * pack + h < len(fields):
                    tile = jnp.where(block_of == h, fields[m * pack + h], tile)
            send[:, m] = tile.reshape(lon, 8, nk)

    def start_panel(sweep):
        def one(k, carry):
            panel_copy(sweep, distant(k), l).start()
            return carry

        lax.fori_loop(0, lon, one, 0)

    def wait_halos(sweep):
        pl.when(has["e"])(lambda: lon_copy(sweep, 0).wait_recv())
        pl.when(has["w"])(lambda: lon_copy(sweep, 1).wait_recv())
        pl.when(has["s"])(lambda: colat_copy(sweep, 0).wait_recv())
        pl.when(has["n"])(lambda: colat_copy(sweep, 1).wait_recv())

    def wait_panel(sweep):
        def one(k, carry):
            panel_copy(sweep, k, k).wait_recv()
            return carry

        lax.fori_loop(0, lon, one, 0)

    def wait_sent(sweep):
        pl.when(has["n"])(lambda: colat_copy(sweep, 0).wait_send())
        pl.when(has["s"])(lambda: colat_copy(sweep, 1).wait_send())
        pl.when(has["w"])(lambda: lon_copy(sweep, 0).wait_send())
        pl.when(has["e"])(lambda: lon_copy(sweep, 1).wait_send())

        def one(k, carry):
            panel_copy(sweep, k, l).wait_send()
            return carry

        lax.fori_loop(0, lon, one, 0)

    def placing():
        m, h = 5 // pack, 5 % pack
        tile = recv1[:, m].reshape(packed, nk)
        ids = jnp.where(block_of == h, tile, 0.0).reshape(lon, 8, nk)
        total = ids
        for turn in range(1, pack):
            total = total + pltpu.roll(ids, turn * slots, 1)
        total = total.reshape(packed, nk)
        blocks = []
        for h in range(pack):
            place = lax.broadcasted_iota(jnp.int32, (packed, ghosts), 1).astype(jnp.float32) + 1.0
            hit = (total[:, :ghosts] == place) & (block_of[:, :ghosts] == h)
            blocks.append(jnp.where(hit, 1.0, 0.0))
        return jnp.concatenate(blocks, axis=1).astype(jnp.bfloat16)

    def place_halos(sweep):
        pad = pads[sweep]

        @pl.when(has["w"])
        def _():
            for f in range(counts[sweep]):
                pad[f, 1 : tc + 1, LEFT - 1, :] = lon_recv[sweep, 1, f]

        @pl.when(has["e"])
        def _():
            for f in range(counts[sweep]):
                pad[f, 1 : tc + 1, LEFT + ac, :] = lon_recv[sweep, 0, f]

    def assemble(sweep, where_to):
        pad, recv, n = pads[sweep], recvs[sweep], counts[sweep]
        sides, bands = [], []
        for m in range(recv.shape[1]):
            if m * pack >= n:
                continue
            rest = recv[:, m].reshape(packed, nk)
            placed = None
            for _ in range(3):
                part = rest.astype(jnp.bfloat16)
                rest = rest - part.astype(jnp.float32)
                term = lax.dot_general(
                    where_to,
                    part,
                    (((0,), (0,)), ((), ())),
                    preferred_element_type=jnp.float32,
                )
                placed = term if placed is None else placed + term
            for h in range(pack):
                if m * pack + h < n:
                    mine = placed[h * ghosts : (h + 1) * ghosts]
                    sides.append(mine[:tc])
                    bands.append(mine[tc:])

        @pl.when(c == 0)
        def _():
            for f in range(n):
                pad[f, 0, inner, :] = bands[f]

        @pl.when(c == colat - 1)
        def _():
            for f in range(n):
                pad[f, tc + 1, inner, :] = bands[f]

        @pl.when(l == 0)
        def _():
            for f in range(n):
                pad[f, 1 : tc + 1, LEFT - 1, :] = sides[f]

        @pl.when(l == lon - 1)
        def _():
            for f in range(n):
                pad[f, 1 : tc + 1, LEFT + ac, :] = sides[f]

    lane = radial(nk)
    top, bottom, inv = lane["top"], lane["bottom"], lane["inv"]

    def first(t, nt, j, nj):
        rows_t, cols = pl.ds(t, nt), pl.ds(j, nj)
        scalar = lambda i: jnp.concatenate(
            [
                jnp.full((1, 1, nk), polar_ref[(c * tc + t + k) * SCALARS + i], jnp.float32)
                for k in range(nt)
            ],
            axis=0,
        )
        inv2 = inv * inv
        near = lambda dt, dj: pad1[4, pl.ds(t + 1 + dt, nt), pl.ds(LEFT + j + dj, nj), :]
        e = near(0, 0)
        a_up = (e + jnp.where(top, e, above(e))) * lane["up_geo"]
        a_dn = (e + jnp.where(bottom, e, below(e))) * lane["down_geo"]
        a_n = (e + near(-1, 0)) * (scalar(0) * inv2)
        a_s = (e + near(1, 0)) * (scalar(1) * inv2)
        h2 = scalar(2) * inv2
        a_w = (e + pad1[4, pl.ds(t + 1, nt), west(j, nj), :]) * h2
        a_e = (e + pad1[4, pl.ds(t + 1, nt), east(j, nj), :]) * h2
        d = OMEGA_VELOCITY / (a_up + a_dn + a_n + a_s + a_w + a_e)
        factors = [
            jnp.where(top, 0.0, a_up * d),
            jnp.where(bottom, 0.0, a_dn * d),
            a_n * d,
            a_s * d,
            a_w * d,
            a_e * d,
            d,
            OMEGA_PRESSURE * e,
            heat[rows_t, cols, :] * d,
        ]
        steps = [scalar(i) * inv for i in (3, 4, 5, 6)]
        for i, factor in enumerate(factors):
            coef[i, rows_t, cols, :] = factor
        for i, step in enumerate(steps):
            geo[i, rows_t] = jnp.broadcast_to(step, (nt, 8, nk))
        for f, value in enumerate(smoothed(pad1, t, nt, j, nj, lane, factors, steps)):
            pad2[f, pl.ds(t + 1, nt), pl.ds(LEFT + j, nj), :] = value

    def second(t, nt, j, nj):
        rows_t, cols = pl.ds(t, nt), pl.ds(j, nj)
        factors = [coef[i, rows_t, cols, :] for i in range(9)]
        steps = [geo[i, rows_t, 0:1, :] for i in range(4)]
        new = smoothed(pad2, t, nt, j, nj, lane, factors, steps)
        for f in range(3):
            vel[f, rows_t, cols, :] = new[f]
        pres[rows_t, cols, :] = new[3]

    def everywhere(update):
        def row(t, carry):
            update(t, 1, 0, ac)
            return carry

        lax.fori_loop(0, tc, row, 0, unroll=2)

    def beside_ghosts(update):
        pl.when(c == 0)(lambda: update(0, 1, 0, ac))
        pl.when(c == colat - 1)(lambda: update(tc - 1, 1, 0, ac))
        pl.when(l == 0)(lambda: update(0, tc, 0, 8))
        pl.when(l == lon - 1)(lambda: update(0, tc, ac - 8, 8))

    greeted = lon + sum(has[side].astype(jnp.int32) for side in "wens")
    for copy in local:
        copy.wait()
    gather(0)
    stage_lon(0)
    pl.semaphore_wait(barrier, greeted)
    start_panel(0)
    start_halos(0)
    wait_halos(0)
    place_halos(0)
    everywhere(first)
    wait_panel(0)
    where_to = placing()
    assemble(0, where_to)
    beside_ghosts(first)
    gather(1)
    start_panel(1)
    stage_lon(1)
    start_halos(1)
    wait_halos(1)
    place_halos(1)
    everywhere(second)
    wait_panel(1)
    assemble(1, where_to)
    beside_ghosts(second)
    wait_sent(0)
    wait_sent(1)


def body(lon, colat, flow, pres, visc, heat, portion, slot, weights, angle):
    tc, ac, nk = flow.shape[2:]
    rows = portion.shape[1]
    pair_rows = (tc + ac + lon - 1) // lon
    slots = 1
    while slots < pair_rows:
        slots *= 2
    pack = 8 // slots
    tiles1, tiles2 = -(-6 // pack), -(-4 // pack)
    f32, i32 = jnp.float32, jnp.int32
    vmem = pl.BlockSpec(memory_space=pltpu.VMEM)
    hbm = pl.BlockSpec(memory_space=pltpu.HBM)
    wide = LEFT + ac + 8
    polar = jnp.asarray(polar_constants(tc, ac, lon, colat))
    constants = jnp.asarray(row_constants(tc, ac, lon, colat))
    vel_new, pres_new = pl.pallas_call(
        functools.partial(kernel, (tc, ac, nk, lon, colat, slots, pack)),
        out_shape=(
            jax.ShapeDtypeStruct(flow.shape[1:], f32),
            jax.ShapeDtypeStruct(pres.shape[1:], f32),
        ),
        in_specs=[hbm] * 10,
        out_specs=(vmem, vmem),
        scratch_shapes=[
            pltpu.VMEM((4, tc + 2, wide, nk), f32),
            pltpu.VMEM((9, tc, ac, nk), f32),
            pltpu.VMEM((4, tc, 8, nk), f32),
            pltpu.VMEM((5, tc + 2, wide, nk), f32),
            pltpu.VMEM((tc, ac, nk), f32),
            pltpu.SMEM(polar.shape, f32),
            pltpu.VMEM(constants.shape, i32),
            pltpu.VMEM(portion.shape, i32),
            pltpu.VMEM(slot.shape, i32),
            pltpu.VMEM(weights.shape, f32),
            pltpu.VMEM(angle.shape, f32),
            pltpu.VMEM((2, 2, 5, tc, nk), f32),
            pltpu.VMEM((2, 2, 5, tc, nk), f32),
            pltpu.VMEM((lon, tiles1, 8, nk), f32),
            pltpu.VMEM((lon, tiles2, 8, nk), f32),
            pltpu.VMEM((lon, tiles1, 8, nk), f32),
            pltpu.VMEM((lon, tiles2, 8, nk), f32),
            pltpu.SemaphoreType.DMA((10,)),
            pltpu.SemaphoreType.DMA((2, 2)),
            pltpu.SemaphoreType.DMA((2, 2)),
            pltpu.SemaphoreType.DMA((2, 2)),
            pltpu.SemaphoreType.DMA((2, 2)),
            pltpu.SemaphoreType.DMA((2, lon)),
            pltpu.SemaphoreType.DMA((2, lon)),
        ],
        compiler_params=pltpu.CompilerParams(
            collective_id=0, has_side_effects=True, vmem_limit_bytes=32 * 1024 * 1024
        ),
    )(*(pltpu.with_memory_space_constraint(x, pltpu.HBM) for x in (polar, constants, portion, slot, weights, angle, flow, pres, visc, heat)))
    return pl.pallas_call(
        copy_out,
        out_shape=(jax.ShapeDtypeStruct(flow.shape, f32), jax.ShapeDtypeStruct(pres.shape, f32)),
        in_specs=[vmem] * 2,
        out_specs=(hbm, hbm),
        scratch_shapes=[pltpu.SemaphoreType.DMA((4,))],
        compiler_params=pltpu.CompilerParams(vmem_limit_bytes=32 * 1024 * 1024),
    )(vel_new, pres_new)


def solution(mesh):
    return jax.shard_map(
        functools.partial(body, mesh.shape["lon"], mesh.shape["colat"]),
        mesh=mesh,
        in_specs=(
            P("panel", None, "colat", "lon", None),
            P("panel", "colat", "lon", None),
            P("panel", "colat", "lon", None),
            P("panel", "colat", "lon", None),
            P("panel", None),
            P("panel", None),
            P("panel", None, None),
            P("panel", None),
        ),
        out_specs=(P("panel", None, "colat", "lon", None), P("panel", "colat", "lon", None)),
        check_vma=False,
    )
```

```python
import functools
import math

import jax
import jax.numpy as jnp
import numpy as np
from jax import lax
from jax.experimental import pallas as pl
from jax.experimental.pallas import tpu as pltpu
from jax.sharding import PartitionSpec as P

OMEGA_VELOCITY = 0.8
OMEGA_PRESSURE = 0.1
INNER_RATIO = 11.0 / 9.0
LEFT = 8
HIGHEST = lax.Precision.HIGHEST
SCALARS = 8


def row_constants(tc, ac, lon, colat):
    pt, at = tc * colat, ac * lon
    rows = np.arange(2 * pt + 2 * at)
    side = rows < 2 * pt
    off = rows - 2 * pt
    group = np.where(side, rows % pt // tc, np.where(off < at, 0, colat - 1))
    target = np.where(rows < pt, 0, np.where(side, lon - 1, off % at // ac))
    place = np.where(side, rows % tc, tc + off % at % ac)
    return np.stack([target, group, place + 1]).astype(np.int32)


def polar_constants(tc, ac, lon, colat):
    pt, at = tc * colat, ac * lon
    dth, dph = 0.5 * math.pi / pt, 1.5 * math.pi / at
    th = 0.25 * math.pi + (np.arange(pt, dtype=np.float64) + 0.5) * dth
    s = np.sin(th)
    table = np.zeros((pt, SCALARS))
    table[:, 0] = 0.5 * np.sin(th - 0.5 * dth) / s / dth**2
    table[:, 1] = 0.5 * np.sin(th + 0.5 * dth) / s / dth**2
    table[:, 2] = 0.5 / (s * dph) ** 2
    table[:, 3] = 0.5 / dth
    table[:, 4] = 0.5 / (s * dph)
    table[:, 5] = np.sin(th - dth) / (2 * dth * s)
    table[:, 6] = np.sin(th + dth) / (2 * dth * s)
    return table.reshape(-1).astype(np.float32)


def above(x):
    return pltpu.roll(x, x.shape[2] - 1, 2)


def below(x):
    return pltpu.roll(x, 1, 2)


def west(j, nj):
    return pl.ds(LEFT + j - 1, nj)


def east(j, nj):
    return pl.ds(LEFT + j + 1, nj)


def radial(nk):
    lane = lax.broadcasted_iota(jnp.int32, (1, 1, nk), 2)
    radius = INNER_RATIO * nk + lane.astype(jnp.float32) + 0.5
    inv = 1.0 / radius
    top, bottom = lane == nk - 1, lane == 0
    return {
        "inv": inv,
        "top": top,
        "bottom": bottom,
        "up_geo": 0.5 * ((radius + 0.5) * inv) ** 2,
        "down_geo": 0.5 * ((radius - 0.5) * inv) ** 2,
        "grad_up": jnp.where(top, 0.0, 0.5),
        "grad_down": jnp.where(bottom, 0.0, 0.5),
        "div_up": jnp.where(top, 0.0, 0.5 * ((radius + 1.0) * inv) ** 2),
        "div_down": jnp.where(bottom, 0.0, 0.5 * ((radius - 1.0) * inv) ** 2),
    }


def smoothed(pad, t, nt, j, nj, lane, factors, steps):
    b_up, b_dn, b_n, b_s, b_w, b_e, d, e, heat = factors
    polar, azimuth, div_n, div_s = steps
    here, cols = pl.ds(t + 1, nt), pl.ds(LEFT + j, nj)

    def near(f):
        return (
            pad[f, here, cols, :],
            pad[f, pl.ds(t, nt), cols, :],
            pad[f, pl.ds(t + 2, nt), cols, :],
            pad[f, here, west(j, nj), :],
            pad[f, here, east(j, nj), :],
        )

    pc, pn, ps, pw, pe = near(3)
    forcing = (
        heat - d * (lane["grad_up"] * above(pc) - lane["grad_down"] * below(pc)),
        d * ((pn - ps) * polar),
        d * ((pw - pe) * azimuth),
    )
    new, div = [], None
    for f in range(3):
        w, wn, ws, ww, we = near(f)
        wu, wd = above(w), below(w)
        total = b_up * wu + b_dn * wd + b_n * wn + b_s * ws + b_w * ww + b_e * we
        new.append((1.0 - OMEGA_VELOCITY) * w + (total + forcing[f]))
        if f == 0:
            div = lane["div_up"] * wu - lane["div_down"] * wd
        elif f == 1:
            div = div + (div_s * ws - div_n * wn)
        else:
            div = div + (we - ww) * azimuth
    new.append(pc - e * div)
    return new


def copy_out(vel, pres, vel_hbm, pres_hbm, sem):
    copies = [pltpu.make_async_copy(vel.at[f], vel_hbm.at[0, f], sem.at[f]) for f in range(3)]
    copies.append(pltpu.make_async_copy(pres, pres_hbm.at[0], sem.at[3]))
    for copy in copies:
        copy.start()
    for copy in copies:
        copy.wait()


def kernel(
    dims,
    polar_hbm,
    const_hbm,
    portion_hbm,
    slot_hbm,
    weight_hbm,
    angle_hbm,
    flow_hbm,
    pres_hbm,
    visc_hbm,
    heat_hbm,
    vel,
    pres,
    pad2,
    coef,
    geo,
    pad1,
    heat,
    polar_ref,
    const_ref,
    portion_ref,
    slot_ref,
    weight_ref,
    angle_ref,
    lon_send,
    lon_recv,
    send1,
    send2,
    recv1,
    recv2,
    in_sem,
    lon_ssem,
    lon_rsem,
    col_ssem,
    col_rsem,
    pan_ssem,
    pan_rsem,
):
    tc, ac, nk, lon, colat, slots, pack = dims
    rows = const_ref.shape[1]
    cells = tc * ac
    ghosts = tc + ac
    packed = 8 * lon
    p = lax.axis_index("panel")
    l = lax.axis_index("lon")
    c = lax.axis_index("colat")
    other = 1 - p
    inner = pl.ds(LEFT, ac)
    pads, sends, recvs, counts = (pad1, pad2), (send1, send2), (recv1, recv2), (5, 4)

    local = [
        pltpu.make_async_copy(flow_hbm.at[0], pad1.at[0:3, 1 : tc + 1, inner, :], in_sem.at[0]),
        pltpu.make_async_copy(pres_hbm.at[0], pad1.at[3, 1 : tc + 1, inner, :], in_sem.at[1]),
        pltpu.make_async_copy(visc_hbm.at[0], pad1.at[4, 1 : tc + 1, inner, :], in_sem.at[2]),
        pltpu.make_async_copy(heat_hbm.at[0], heat, in_sem.at[3]),
        pltpu.make_async_copy(polar_hbm, polar_ref, in_sem.at[4]),
    ]
    tables = [
        pltpu.make_async_copy(const_hbm, const_ref, in_sem.at[5]),
        pltpu.make_async_copy(portion_hbm, portion_ref, in_sem.at[6]),
        pltpu.make_async_copy(slot_hbm, slot_ref, in_sem.at[7]),
        pltpu.make_async_copy(weight_hbm, weight_ref, in_sem.at[8]),
        pltpu.make_async_copy(angle_hbm, angle_ref, in_sem.at[9]),
    ]

    barrier = pltpu.get_barrier_semaphore()

    def distant(k):
        return l ^ (lon - 1 - k) if lon & (lon - 1) == 0 else lax.rem(l + k, lon)

    def greet(**where):
        pl.semaphore_signal(
            barrier, inc=1, device_id=where, device_id_type=pl.DeviceIdType.MESH
        )

    def greet_panel(k, carry):
        greet(panel=other, lon=distant(k))
        return carry

    lax.fori_loop(0, lon, greet_panel, 0)
    has = {"w": l > 0, "e": l < lon - 1, "n": c > 0, "s": c < colat - 1}
    pl.when(has["w"])(lambda: greet(lon=l - 1))
    pl.when(has["e"])(lambda: greet(lon=l + 1))
    pl.when(has["n"])(lambda: greet(colat=c - 1))
    pl.when(has["s"])(lambda: greet(colat=c + 1))

    for copy in tables + local:
        copy.start()
    for copy in tables:
        copy.wait()

    target = const_ref[0:1, :]
    serving = (portion_ref[...] == l) & (const_ref[1:2, :] == c)
    wanted = jnp.where(serving, target, -1)
    lon_iota = lax.broadcasted_iota(jnp.int32, (lon, rows), 0)
    member = wanted == lon_iota
    member_f = member.astype(jnp.float32)
    before = (
        lax.broadcasted_iota(jnp.int32, (rows, rows), 0)
        < lax.broadcasted_iota(jnp.int32, (rows, rows), 1)
    ).astype(jnp.float32)
    running = jnp.dot(
        member_f.astype(jnp.bfloat16),
        before.astype(jnp.bfloat16),
        preferred_element_type=jnp.float32,
    )
    rank = jnp.sum(jnp.where(member, running, 0.0), axis=0, keepdims=True)
    key = jnp.where(serving, target.astype(jnp.float32) * slots + rank, -1.0)
    key = jnp.where(rank < slots, key, -1.0)
    line = lax.broadcasted_iota(jnp.int32, (packed, rows), 0)
    line_key = (line >> 3) * slots + (line & (slots - 1))
    chosen = key == line_key.astype(jnp.float32)

    def picked(values):
        return jnp.sum(jnp.where(chosen, values, 0.0), axis=1, keepdims=True)

    angle = angle_ref[...]
    donor = picked(slot_ref[...].astype(jnp.float32))
    frac_t = picked(weight_ref[0, 0:1, :])
    frac_j = picked(weight_ref[0, 1:2, :])
    cosine = picked(jnp.cos(angle))
    sine = picked(jnp.sin(angle))
    ghost_id = picked(const_ref[2:3, :].astype(jnp.float32))
    used = jnp.where(ghost_id > 0.5, 1.0, 0.0)
    step = lax.broadcasted_iota(jnp.int32, (packed, cells), 1).astype(jnp.float32) - donor
    keep_t = (1.0 - frac_t) * used
    lean_t = frac_t * used
    blend = jnp.where(step == 0.0, keep_t * (1.0 - frac_j), 0.0)
    blend = jnp.where(step == 1.0, keep_t * frac_j, blend)
    blend = jnp.where(step == float(ac), lean_t * (1.0 - frac_j), blend)
    blend = jnp.where(step == float(ac + 1), lean_t * frac_j, blend)
    block_of = (
        (lax.broadcasted_iota(jnp.int32, (packed, nk), 0) & 7) >> (slots.bit_length() - 1)
    )

    def lon_copy(sweep, side):
        n = counts[sweep]
        return pltpu.make_async_remote_copy(
            src_ref=lon_send.at[sweep, side, 0:n],
            dst_ref=lon_recv.at[sweep, side, 0:n],
            send_sem=lon_ssem.at[sweep, side],
            recv_sem=lon_rsem.at[sweep, side],
            device_id={"lon": jnp.maximum(l - 1, 0) if side == 0 else jnp.minimum(l + 1, lon - 1)},
            device_id_type=pl.DeviceIdType.MESH,
        )

    def colat_copy(sweep, side):
        pad = pads[sweep]
        from_row, to_row = (1, tc + 1) if side == 0 else (tc, 0)
        return pltpu.make_async_remote_copy(
            src_ref=pad.at[:, from_row, inner, :],
            dst_ref=pad.at[:, to_row, inner, :],
            send_sem=col_ssem.at[sweep, side],
            recv_sem=col_rsem.at[sweep, side],
            device_id={"colat": jnp.maximum(c - 1, 0) if side == 0 else jnp.minimum(c + 1, colat - 1)},
            device_id_type=pl.DeviceIdType.MESH,
        )

    def panel_copy(sweep, to, slot):
        return pltpu.make_async_remote_copy(
            src_ref=sends[sweep].at[to],
            dst_ref=recvs[sweep].at[slot],
            send_sem=pan_ssem.at[sweep, to],
            recv_sem=pan_rsem.at[sweep, slot],
            device_id={"panel": other, "lon": to},
            device_id_type=pl.DeviceIdType.MESH,
        )

    def stage_lon(sweep):
        pad = pads[sweep]
        for f in range(counts[sweep]):
            lon_send[sweep, 0, f] = pad[f, 1 : tc + 1, LEFT, :]
            lon_send[sweep, 1, f] = pad[f, 1 : tc + 1, LEFT + ac - 1, :]

    def start_halos(sweep):
        pl.when(has["n"])(lambda: colat_copy(sweep, 0).start())
        pl.when(has["s"])(lambda: colat_copy(sweep, 1).start())
        pl.when(has["w"])(lambda: lon_copy(sweep, 0).start())
        pl.when(has["e"])(lambda: lon_copy(sweep, 1).start())

    def gather(sweep):
        pad, send, n = pads[sweep], sends[sweep], counts[sweep]
        donors = [pad[f, 1 : tc + 1, inner, :].reshape(cells, nk) for f in range(n)]
        blended = jnp.dot(
            blend,
            jnp.concatenate(donors, axis=1),
            precision=HIGHEST,
            preferred_element_type=jnp.float32,
        )
        fields = [blended[:, f * nk : (f + 1) * nk] for f in range(n)]
        polar, azimuth = fields[1], fields[2]
        fields[1] = cosine * polar + sine * azimuth
        fields[2] = cosine * azimuth - sine * polar
        if sweep == 0:
            fields.append(jnp.broadcast_to(ghost_id, (packed, nk)))
        for m in range(send.shape[1]):
            tile = jnp.zeros((packed, nk), jnp.float32)
            for h in range(pack):
                if m * pack + h < len(fields):
                    tile = jnp.where(block_of == h, fields[m * pack + h], tile)
            send[:, m] = tile.reshape(lon, 8, nk)

    def start_panel(sweep):
        def one(k, carry):
            panel_copy(sweep, distant(k), l).start()
            return carry

        lax.fori_loop(0, lon, one, 0)

    def wait_halos(sweep):
        pl.when(has["e"])(lambda: lon_copy(sweep, 0).wait_recv())
        pl.when(has["w"])(lambda: lon_copy(sweep, 1).wait_recv())
        pl.when(has["s"])(lambda: colat_copy(sweep, 0).wait_recv())
        pl.when(has["n"])(lambda: colat_copy(sweep, 1).wait_recv())

    def wait_panel(sweep):
        def one(k, carry):
            panel_copy(sweep, k, k).wait_recv()
            return carry

        lax.fori_loop(0, lon, one, 0)

    def wait_sent(sweep):
        pl.when(has["n"])(lambda: colat_copy(sweep, 0).wait_send())
        pl.when(has["s"])(lambda: colat_copy(sweep, 1).wait_send())
        pl.when(has["w"])(lambda: lon_copy(sweep, 0).wait_send())
        pl.when(has["e"])(lambda: lon_copy(sweep, 1).wait_send())

        def one(k, carry):
            panel_copy(sweep, k, l).wait_send()
            return carry

        lax.fori_loop(0, lon, one, 0)

    def placing():
        m, h = 5 // pack, 5 % pack
        tile = recv1[:, m].reshape(packed, nk)
        ids = jnp.where(block_of == h, tile, 0.0).reshape(lon, 8, nk)
        total = ids
        for turn in range(1, pack):
            total = total + pltpu.roll(ids, turn * slots, 1)
        total = total.reshape(packed, nk)
        blocks = []
        for h in range(pack):
            place = lax.broadcasted_iota(jnp.int32, (packed, ghosts), 1).astype(jnp.float32) + 1.0
            hit = (total[:, :ghosts] == place) & (block_of[:, :ghosts] == h)
            blocks.append(jnp.where(hit, 1.0, 0.0))
        return jnp.concatenate(blocks, axis=1).astype(jnp.bfloat16)

    def place_halos(sweep):
        pad = pads[sweep]

        @pl.when(has["w"])
        def _():
            for f in range(counts[sweep]):
                pad[f, 1 : tc + 1, LEFT - 1, :] = lon_recv[sweep, 1, f]

        @pl.when(has["e"])
        def _():
            for f in range(counts[sweep]):
                pad[f, 1 : tc + 1, LEFT + ac, :] = lon_recv[sweep, 0, f]

    def assemble(sweep, where_to):
        pad, recv, n = pads[sweep], recvs[sweep], counts[sweep]
        sides, bands = [], []
        tiles = -(-n // pack)
        rest = jnp.concatenate([recv[:, m].reshape(packed, nk) for m in range(tiles)], axis=1)
        every = None
        for _ in range(3):
            part = rest.astype(jnp.bfloat16)
            rest = rest - part.astype(jnp.float32)
            term = lax.dot_general(
                where_to,
                part,
                (((0,), (0,)), ((), ())),
                preferred_element_type=jnp.float32,
            )
            every = term if every is None else every + term
        for m in range(tiles):
            placed = every[:, m * nk : (m + 1) * nk]
            for h in range(pack):
                if m * pack + h < n:
                    mine = placed[h * ghosts : (h + 1) * ghosts]
                    sides.append(mine[:tc])
                    bands.append(mine[tc:])

        @pl.when(c == 0)
        def _():
            for f in range(n):
                pad[f, 0, inner, :] = bands[f]

        @pl.when(c == colat - 1)
        def _():
            for f in range(n):
                pad[f, tc + 1, inner, :] = bands[f]

        @pl.when(l == 0)
        def _():
            for f in range(n):
                pad[f, 1 : tc + 1, LEFT - 1, :] = sides[f]

        @pl.when(l == lon - 1)
        def _():
            for f in range(n):
                pad[f, 1 : tc + 1, LEFT + ac, :] = sides[f]

    lane = radial(nk)
    top, bottom, inv = lane["top"], lane["bottom"], lane["inv"]

    def first(t, nt, j, nj):
        rows_t, cols = pl.ds(t, nt), pl.ds(j, nj)
        scalar = lambda i: jnp.concatenate(
            [
                jnp.full((1, 1, nk), polar_ref[(c * tc + t + k) * SCALARS + i], jnp.float32)
                for k in range(nt)
            ],
            axis=0,
        )
        inv2 = inv * inv
        near = lambda dt, dj: pad1[4, pl.ds(t + 1 + dt, nt), pl.ds(LEFT + j + dj, nj), :]
        e = near(0, 0)
        a_up = (e + jnp.where(top, e, above(e))) * lane["up_geo"]
        a_dn = (e + jnp.where(bottom, e, below(e))) * lane["down_geo"]
        a_n = (e + near(-1, 0)) * (scalar(0) * inv2)
        a_s = (e + near(1, 0)) * (scalar(1) * inv2)
        h2 = scalar(2) * inv2
        a_w = (e + pad1[4, pl.ds(t + 1, nt), west(j, nj), :]) * h2
        a_e = (e + pad1[4, pl.ds(t + 1, nt), east(j, nj), :]) * h2
        d = OMEGA_VELOCITY / (a_up + a_dn + a_n + a_s + a_w + a_e)
        factors = [
            jnp.where(top, 0.0, a_up * d),
            jnp.where(bottom, 0.0, a_dn * d),
            a_n * d,
            a_s * d,
            a_w * d,
            a_e * d,
            d,
            OMEGA_PRESSURE * e,
            heat[rows_t, cols, :] * d,
        ]
        steps = [scalar(i) * inv for i in (3, 4, 5, 6)]
        for i, factor in enumerate(factors):
            coef[i, rows_t, cols, :] = factor
        for i, step in enumerate(steps):
            geo[i, rows_t] = jnp.broadcast_to(step, (nt, 8, nk))
        for f, value in enumerate(smoothed(pad1, t, nt, j, nj, lane, factors, steps)):
            pad2[f, pl.ds(t + 1, nt), pl.ds(LEFT + j, nj), :] = value

    def second(t, nt, j, nj):
        rows_t, cols = pl.ds(t, nt), pl.ds(j, nj)
        factors = [coef[i, rows_t, cols, :] for i in range(9)]
        steps = [geo[i, rows_t, 0:1, :] for i in range(4)]
        new = smoothed(pad2, t, nt, j, nj, lane, factors, steps)
        for f in range(3):
            vel[f, rows_t, cols, :] = new[f]
        pres[rows_t, cols, :] = new[3]

    def everywhere(update):
        def row(t, carry):
            update(t, 1, 0, ac)
            return carry

        lax.fori_loop(0, tc, row, 0, unroll=2)

    def beside_ghosts(update):
        pl.when(c == 0)(lambda: update(0, 1, 0, ac))
        pl.when(c == colat - 1)(lambda: update(tc - 1, 1, 0, ac))
        pl.when(l == 0)(lambda: update(0, tc, 0, 8))
        pl.when(l == lon - 1)(lambda: update(0, tc, ac - 8, 8))

    greeted = lon + sum(has[side].astype(jnp.int32) for side in "wens")
    for copy in local:
        copy.wait()
    gather(0)
    stage_lon(0)
    pl.semaphore_wait(barrier, greeted)
    start_panel(0)
    start_halos(0)
    wait_halos(0)
    place_halos(0)
    everywhere(first)
    wait_panel(0)
    where_to = placing()
    assemble(0, where_to)
    beside_ghosts(first)
    gather(1)
    start_panel(1)
    stage_lon(1)
    start_halos(1)
    wait_halos(1)
    place_halos(1)
    everywhere(second)
    wait_panel(1)
    assemble(1, where_to)
    beside_ghosts(second)
    wait_sent(0)
    wait_sent(1)


def body(lon, colat, flow, pres, visc, heat, portion, slot, weights, angle):
    tc, ac, nk = flow.shape[2:]
    rows = portion.shape[1]
    pair_rows = (tc + ac + lon - 1) // lon
    slots = 1
    while slots < pair_rows:
        slots *= 2
    pack = 8 // slots
    tiles1, tiles2 = -(-6 // pack), -(-4 // pack)
    f32, i32 = jnp.float32, jnp.int32
    vmem = pl.BlockSpec(memory_space=pltpu.VMEM)
    hbm = pl.BlockSpec(memory_space=pltpu.HBM)
    wide = LEFT + ac + 8
    polar = jnp.asarray(polar_constants(tc, ac, lon, colat))
    constants = jnp.asarray(row_constants(tc, ac, lon, colat))
    vel_new, pres_new = pl.pallas_call(
        functools.partial(kernel, (tc, ac, nk, lon, colat, slots, pack)),
        out_shape=(
            jax.ShapeDtypeStruct(flow.shape[1:], f32),
            jax.ShapeDtypeStruct(pres.shape[1:], f32),
        ),
        in_specs=[hbm] * 10,
        out_specs=(vmem, vmem),
        scratch_shapes=[
            pltpu.VMEM((4, tc + 2, wide, nk), f32),
            pltpu.VMEM((9, tc, ac, nk), f32),
            pltpu.VMEM((4, tc, 8, nk), f32),
            pltpu.VMEM((5, tc + 2, wide, nk), f32),
            pltpu.VMEM((tc, ac, nk), f32),
            pltpu.SMEM(polar.shape, f32),
            pltpu.VMEM(constants.shape, i32),
            pltpu.VMEM(portion.shape, i32),
            pltpu.VMEM(slot.shape, i32),
            pltpu.VMEM(weights.shape, f32),
            pltpu.VMEM(angle.shape, f32),
            pltpu.VMEM((2, 2, 5, tc, nk), f32),
            pltpu.VMEM((2, 2, 5, tc, nk), f32),
            pltpu.VMEM((lon, tiles1, 8, nk), f32),
            pltpu.VMEM((lon, tiles2, 8, nk), f32),
            pltpu.VMEM((lon, tiles1, 8, nk), f32),
            pltpu.VMEM((lon, tiles2, 8, nk), f32),
            pltpu.SemaphoreType.DMA((10,)),
            pltpu.SemaphoreType.DMA((2, 2)),
            pltpu.SemaphoreType.DMA((2, 2)),
            pltpu.SemaphoreType.DMA((2, 2)),
            pltpu.SemaphoreType.DMA((2, 2)),
            pltpu.SemaphoreType.DMA((2, lon)),
            pltpu.SemaphoreType.DMA((2, lon)),
        ],
        compiler_params=pltpu.CompilerParams(
            collective_id=0, has_side_effects=True, vmem_limit_bytes=32 * 1024 * 1024
        ),
    )(*(pltpu.with_memory_space_constraint(x, pltpu.HBM) for x in (polar, constants, portion, slot, weights, angle, flow, pres, visc, heat)))
    return pl.pallas_call(
        copy_out,
        out_shape=(jax.ShapeDtypeStruct(flow.shape, f32), jax.ShapeDtypeStruct(pres.shape, f32)),
        in_specs=[vmem] * 2,
        out_specs=(hbm, hbm),
        scratch_shapes=[pltpu.SemaphoreType.DMA((4,))],
        compiler_params=pltpu.CompilerParams(vmem_limit_bytes=32 * 1024 * 1024),
    )(vel_new, pres_new)


def solution(mesh):
    return jax.shard_map(
        functools.partial(body, mesh.shape["lon"], mesh.shape["colat"]),
        mesh=mesh,
        in_specs=(
            P("panel", None, "colat", "lon", None),
            P("panel", "colat", "lon", None),
            P("panel", "colat", "lon", None),
            P("panel", "colat", "lon", None),
            P("panel", None),
            P("panel", None),
            P("panel", None, None),
            P("panel", None),
        ),
        out_specs=(P("panel", None, "colat", "lon", None), P("panel", "colat", "lon", None)),
        check_vma=False,
    )
```
